128 devices in a mesh: sample: 4 (over z_hi, core), expert: 32 (over y, x, z_lo).
Axes of the slice: x: 4, y: 4, z: 4 (z_hi: 2, z_lo: 2; z = z_hi * 2 + z_lo), core: 2. Of those that a mesh axis runs over, the one named last changes fastest.
Arguments:
- tokens: bfloat16 [4, 4096, 2048], P('sample', 'expert'), may hold values from -6 to 6
- routes: int32 [4, 4096, 8], P('sample', 'expert'), may hold values from 0 to 31, all different within a row; in each aligned block of 128 rows (0 to 127, 128 to 255, ..., all dimensions but the last counted through in order) at most 33 rows name the same one
- probs: bfloat16 [4, 4096, 8], P('sample', 'expert'), may hold values from 0.049804688 to 1
- cotangent: bfloat16 [4, 4096, 2048], P('sample', 'expert'), may hold values from -6 to 6
- w_gate_up: bfloat16 [32, 2048, 1536], P('expert'), may hold values from -0.125 to 0.125
- w_down: bfloat16 [32, 768, 2048], P('expert'), may hold values from -0.21875 to 0.21875
- gu_noise: float32 [4, 32, 8, 6], P('sample', 'expert'), may hold values from 0.5 to 1.5
- down_noise: float32 [4, 32, 3, 8], P('sample', 'expert'), may hold values from 0.5 to 1.5
Outputs:
- layer_out: bfloat16 [4, 4096, 2048], P('sample', 'expert')
- input_grad: bfloat16 [4, 4096, 2048], P('sample', 'expert')
- prob_grad: float32 [4, 4096, 8], P('sample', 'expert')
- grad_gate_up: float32 [32, 2048, 1536], P('expert', 'sample')
- grad_down: float32 [32, 768, 2048], P('expert', None, 'sample')
The draws below stay inside these ranges and needn't reach their ends.
Inputs may be any that keep to these rules, and one draw needn't show every extreme that they name: `routes`: each row names 8 different experts. In each aligned block of 128 rows of a group (the tokens of one device) no expert is named more than 33 times, a bound that some block reaches.
All inputs are finite; a program needn't handle non-finite values.
Results may differ from the reference program's by a relative error of at most 0.0083.
Values may be sent and summed in bfloat16 or wider, within the bound.
No kernel may reach another device: no remote copies, remote signals or barrier semaphores. Data moves between devices by JAX's collectives and lax.ppermute only.
A program may use at most 192 MiB of HBM per device.

```python
import math
from functools import partial
import jax
import jax.numpy as jnp
import numpy as np
from jax import lax

D = 2048
FF = 768
TOP = 8
TILE = 256
TOK_DEV = 128
SAMPLES = 4
EXPERTS = 32
GTOK = 4096
CAP = 33
N_EXPERT = 32


def levels(key, extent, pieces, low, high):
    def one(dim, blocks):
        draws = jax.random.uniform(jax.random.fold_in(jax.random.fold_in(key, 6), dim), (blocks,), jnp.float32, low / len(pieces), high / len(pieces))
        return jnp.repeat(jnp.exp(draws), extent[dim] // blocks).reshape((-1,) + (1,) * (len(extent) - dim - 1))

    level = one(*pieces[0])
    for cut in pieces[1:]:
        level = level * one(*cut)
    return level


def routed_block(own_key, own, number, rows, count, top, reach, lean):
    sequence = jax.random.permutation(own_key, count)
    packed, common = load_shares(count, rows * top, reach, lean, True), load_shares(count, rows * top, reach, lean, False)
    places = jnp.arange(count)

    def named(sizes, offset_by):
        used = int((sizes > 0).sum())
        fixed = max(1, used // 4)
        shifted = fixed + (places - fixed + offset_by * (used - fixed)) % max(1, count - fixed)
        return jnp.zeros((count,), jnp.int32).at[sequence[jnp.where(places < fixed, places, shifted)]].set(jnp.asarray(sizes, jnp.int32))

    sizes = jnp.where(number % 4 == 0, named(packed, number // 4), named(common, number - number // 4 - 1))
    mixed = jax.random.permutation(jax.random.fold_in(own, 3), count)
    donor, taker = mixed[0:count // 2 * 2:2], mixed[1:count // 2 * 2:2]
    slack = jnp.minimum(sizes[donor] - 1, reach - sizes[taker]) // 2
    slack = jnp.where((donor == sequence[0]) | (taker == sequence[0]) | (sizes[taker] == 0), 0, jnp.maximum(slack, 0))
    shifted = jax.random.randint(jax.random.fold_in(own, 4), (count // 2,), 0, 1 << 20) % (slack + 1)
    sizes = sizes.at[donor].add(-shifted).at[taker].add(shifted)
    items = jnp.searchsorted(jnp.cumsum(sizes), jnp.arange(rows * top), side="right").astype(jnp.int32)
    grid = items.reshape(top, rows).T
    grid = grid[jax.random.permutation(jax.random.fold_in(own, 1), rows)]
    offset_by = jax.random.randint(jax.random.fold_in(own, 2), (rows, 1), 0, top)
    return jnp.take_along_axis(grid, (jnp.arange(top)[None, :] + offset_by) % top, axis=1)


def load_shares(number_of, total, limit, skew, full):
    portions = [(1 << 20) // math.isqrt(rank ** skew) + 1 for rank in range(1, number_of + 1)]
    largest = limit if full else min(limit, max(-(-total // number_of), total * portions[0] // sum(portions)))
    least = 1 if total - largest >= number_of - 1 else 0
    holding, spare = [largest] + [least] * (number_of - 1), total - largest - least * (number_of - 1)
    while spare > 0:
        movable = [i for i in range(1, number_of) if holding[i] < largest] or [i for i in range(1, number_of) if holding[i] < limit]
        pool, left = sum([portions[i] for i in movable]), spare
        for i in movable:
            extra = min(limit - holding[i], max(1, left * portions[i] // pool), spare)
            holding[i] = holding[i] + extra
            spare = spare - extra
    return np.array(holding)


def centred(rng, dims, scale, most, shards=(), held_as=jnp.bfloat16):
    result = jax.random.normal(rng, dims, jnp.float32) * scale
    if len(shards) > 0:
        result = levels(rng, dims, shards, -0.22, 0.18) * result
    return jnp.clip(result, min=-most, max=most).astype(held_as)


def setup_inputs(seed: int = 0) -> dict:
    streams_of = jax.random.split(jax.random.key(seed), 9)
    tokens = centred(streams_of[0], (SAMPLES, GTOK, D), 1.0, 6.0, ((0, 4), (1, 32)))
    routes_keys = jax.random.split(jax.random.fold_in(streams_of[1], 1), SAMPLES * GTOK // TOK_DEV)
    routes_turns = jax.random.permutation(jax.random.fold_in(streams_of[1], 3), SAMPLES * GTOK // TOK_DEV)
    routes = jax.vmap(lambda own, number: routed_block(jax.random.fold_in(streams_of[1], 2), own, number, TOK_DEV, EXPERTS, TOP, CAP, 1))(routes_keys, routes_turns).reshape((SAMPLES, GTOK, TOP))
    probs = jnp.clip(jnp.exp(math.log(1.0) - 2.9996462 * jax.random.uniform(streams_of[2], (SAMPLES, GTOK, TOP), jnp.float32) ** levels(streams_of[2], (SAMPLES, GTOK, TOP), ((0, 4), (1, 32)), -0.2, 0.2)), 0.049804688, 1.0).astype(jnp.bfloat16)
    cotangent = centred(streams_of[3], (SAMPLES, GTOK, D), 1.0, 6.0, ((0, 4), (1, 32)))
    w_gate_up = centred(streams_of[4], (EXPERTS, D, 2 * FF), D ** -0.5, 0.125, ((0, 32),))
    w_down = centred(streams_of[5], (EXPERTS, FF, D), FF ** -0.5, 0.21875, ((0, 32),))
    gu_noise = jnp.clip(1.0 + 0.1 * jax.random.normal(streams_of[6], (SAMPLES, EXPERTS, D // TILE, 2 * FF // TILE), jnp.float32), 0.5, 1.5)
    down_noise = jnp.clip(1.0 + 0.1 * jax.random.normal(streams_of[7], (SAMPLES, EXPERTS, FF // TILE, D // TILE), jnp.float32), 0.5, 1.5)
    return dict(tokens=tokens, routes=routes, probs=probs, cotangent=cotangent, w_gate_up=w_gate_up, w_down=w_down, gu_noise=gu_noise, down_noise=down_noise)


def tile_scale(weight, noise):
    batch, height, breadth = weight.shape
    tiles_down = noise.shape[1]
    tiles_across = noise.shape[2]
    blocks = weight.astype(jnp.float32).reshape(batch, tiles_down, height // tiles_down, tiles_across, breadth // tiles_across)
    return (blocks * noise[:, :, None, :, None]).reshape(batch, height, breadth)


def slot_table(routes, probs, capacity, experts):
    count, chosen = routes.shape
    flattened = routes.reshape(-1).astype(jnp.int32)
    onehot = (flattened[:, None] == jnp.arange(experts, dtype=jnp.int32)[None, :]).astype(jnp.int32)
    before = (jnp.cumsum(onehot, axis=0) - onehot).astype(jnp.int32)
    slots = jnp.sum(before * onehot, axis=1).astype(jnp.int32)
    position = (flattened * capacity + slots).astype(jnp.int32)
    owner = jnp.arange(count * chosen, dtype=jnp.int32) // chosen
    source = jnp.full((experts * capacity,), count, jnp.int32).at[position].set(owner)
    weights = jnp.zeros((experts * capacity,), probs.dtype).at[position].set(probs.reshape(-1))
    return position.reshape(count, chosen), source, weights


def expert_pass(operands):
    inputs, upstream, weight_in, weight_out = operands
    gate_up = jnp.dot(inputs, weight_in, preferred_element_type=jnp.float32)
    gate = gate_up[:, :FF]
    upward = gate_up[:, FF:]
    hidden = (jax.nn.silu(gate) * upward).astype(jnp.bfloat16)
    output = jnp.dot(hidden, weight_out, preferred_element_type=jnp.float32).astype(jnp.bfloat16)
    grad_hidden = jnp.dot(upstream, weight_out.T, preferred_element_type=jnp.float32)
    sigma = jax.nn.sigmoid(gate)
    slope = sigma * (1.0 + gate * (1.0 - sigma))
    grad_mix = jnp.concatenate([grad_hidden * upward * slope, grad_hidden * gate * sigma], axis=1).astype(jnp.bfloat16)
    grad_input = jnp.dot(grad_mix, weight_in.T, preferred_element_type=jnp.float32).astype(jnp.bfloat16)
    raw_in = jnp.dot(inputs.T, grad_mix, preferred_element_type=jnp.float32)
    raw_out = jnp.dot(hidden.T, upstream, preferred_element_type=jnp.float32)
    return output, grad_input, raw_in, raw_out


def reference(tokens, routes, probs, cotangent, w_gate_up, w_down, gu_noise, down_noise):
    span = N_EXPERT * CAP
    table = jax.vmap(partial(slot_table, capacity=CAP, experts=EXPERTS))
    sum_in = jnp.zeros((EXPERTS, D, 2 * FF), jnp.float32)
    sum_out = jnp.zeros((EXPERTS, FF, D), jnp.float32)
    outputs = []
    in_grads = []
    prob_grads = []
    for group in range(SAMPLES):
        weight_in = tile_scale(w_gate_up, gu_noise[group]).astype(jnp.bfloat16)
        weight_out = tile_scale(w_down, down_noise[group]).astype(jnp.bfloat16)
        position = table(routes[group].reshape(N_EXPERT, TOK_DEV, TOP), probs[group].reshape(N_EXPERT, TOK_DEV, TOP))[0]
        blocks = jnp.arange(N_EXPERT, dtype=jnp.int32)[:, None, None]
        index = ((position // CAP) * span + blocks * CAP + position % CAP).reshape(-1).astype(jnp.int32)
        repeated_x = jnp.repeat(tokens[group], TOP, axis=0)
        prob_flat = probs[group].reshape(-1).astype(jnp.float32)
        repeated_dy = (prob_flat[:, None] * jnp.repeat(cotangent[group], TOP, axis=0).astype(jnp.float32)).astype(jnp.bfloat16)
        buffer_x = jnp.zeros((EXPERTS * span, D), jnp.bfloat16).at[index].set(repeated_x).reshape(EXPERTS, span, D)
        buffer_dy = jnp.zeros((EXPERTS * span, D), jnp.bfloat16).at[index].set(repeated_dy).reshape(EXPERTS, span, D)
        output, grad_input, raw_in, raw_out = lax.map(expert_pass, (buffer_x, buffer_dy, weight_in, weight_out))
        sum_in = sum_in + tile_scale(raw_in, gu_noise[group])
        sum_out = sum_out + tile_scale(raw_out, down_noise[group])
        routed_y = output.reshape(EXPERTS * span, D)[index].reshape(GTOK, TOP, D).astype(jnp.float32)
        routed_dx = grad_input.reshape(EXPERTS * span, D)[index].reshape(GTOK, TOP, D).astype(jnp.float32)
        weights = probs[group].astype(jnp.float32)
        outputs.append(jnp.sum(weights[:, :, None] * routed_y, axis=1).astype(jnp.bfloat16))
        prob_grads.append(jnp.sum(cotangent[group].astype(jnp.float32)[:, None, :] * routed_y, axis=2))
        in_grads.append(jnp.sum(routed_dx, axis=1).astype(jnp.bfloat16))
    return (jnp.stack(outputs), jnp.stack(in_grads), jnp.stack(prob_grads), sum_in / SAMPLES, sum_out / SAMPLES)
```

```python
import functools

import jax
import jax.numpy as jnp
from jax import lax
from jax.experimental import pallas as pl
from jax.experimental.pallas import tpu as pltpu
from jax.sharding import PartitionSpec as P

D = 2048
FF = 768
TOP = 8
TOK = 128
BLOCKS = 32
LANES = 128
COLS = D // LANES
MAIN = 32
PACK = MAIN * COLS + COLS
ROWS = BLOCKS * (MAIN + 1)
BIG = BLOCKS * MAIN
VMEM_LIMIT = 48 * 1024 * 1024

F32 = jnp.float32
BF16 = jnp.bfloat16


def params(**more):
    return pltpu.CompilerParams(vmem_limit_bytes=VMEM_LIMIT, **more)


def cost(flops, moved):
    return pl.CostEstimate(flops=flops, bytes_accessed=moved, transcendentals=0)


def iota(shape, dim):
    return lax.broadcasted_iota(jnp.int32, shape, dim)


def dot(a, b):
    return jnp.dot(a, b, preferred_element_type=F32)


def dot_nt(a, b):
    return lax.dot_general(a, b, (((1,), (1,)), ((), ())), preferred_element_type=F32)


def dot_tn(a, b):
    return lax.dot_general(a, b, (((0,), (0,)), ((), ())), preferred_element_type=F32)


def slot_keys(routes):
    lane = iota((TOK, LANES), 1)
    chosen = jnp.zeros((TOK, LANES), F32)
    for k in range(TOP):
        chosen = jnp.where(routes[:, k : k + 1] == lane, 1.0, chosen)
    earlier = jnp.where(iota((TOK, TOK), 0) > iota((TOK, TOK), 1), 1.0, 0.0).astype(BF16)
    rank = dot(earlier, chosen.astype(BF16))
    return jnp.where(chosen > 0.0, rank, -1.0)


def expert_weights(routes, probs):
    lane = iota((TOK, LANES), 1)
    weight = jnp.zeros((TOK, LANES), F32)
    for k in range(TOP):
        weight = jnp.where(routes[:, k : k + 1] == lane, probs[:, k : k + 1].astype(F32), weight)
    return weight


def last_slot_order(receive):
    count = BLOCKS * COLS
    tile = iota((count, count), 1 if receive else 0)
    row = iota((count, count), 0 if receive else 1)
    same = ((tile // COLS) == (row % BLOCKS)) & ((tile % COLS) == (row // BLOCKS))
    return jnp.where(same, 1.0, 0.0).astype(BF16)


def unpack_last(tile):
    flat = tile.reshape(BLOCKS * COLS, LANES)
    return dot(last_slot_order(True), flat).astype(BF16)


def dispatch_kernel(weighted, routes_ref, probs_ref, value_ref, out_ref, last_ref):
    routes = routes_ref[...]
    key = slot_keys(routes).T
    spread = jnp.where(iota((BIG, LANES), 0) // MAIN == iota((BIG, LANES), 1), 1.0, 0.0).astype(BF16)
    hit = dot(spread, key.astype(BF16)) == (iota((BIG, TOK), 0) % MAIN).astype(F32)
    last_hit = key[:BLOCKS] == float(MAIN)
    if weighted:
        weight = expert_weights(routes, probs_ref[...]).T
        pick = jnp.where(hit, dot(spread, weight.astype(BF16)), 0.0).astype(BF16)
        last_pick = jnp.where(last_hit, weight[:BLOCKS], 0.0).astype(BF16)
    else:
        pick = jnp.where(hit, 1.0, 0.0).astype(BF16)
        last_pick = jnp.where(last_hit, 1.0, 0.0).astype(BF16)
    for j in range(COLS):
        value = value_ref[:, j * LANES : (j + 1) * LANES]
        rows = dot(pick, value).astype(BF16)
        out_ref[:, j * MAIN : (j + 1) * MAIN, :] = rows.reshape(BLOCKS, MAIN, LANES)
        last_ref[j * BLOCKS : (j + 1) * BLOCKS, :] = dot(last_pick, value).astype(BF16)
    tiles = dot(last_slot_order(False), last_ref[...]).astype(BF16)
    out_ref[:, MAIN * COLS :, :] = tiles.reshape(BLOCKS, COLS, LANES)


def dispatch(routes, probs, value, weighted):
    return pl.pallas_call(
        functools.partial(dispatch_kernel, weighted),
        out_shape=jax.ShapeDtypeStruct((BLOCKS, PACK, LANES), BF16),
        scratch_shapes=[pltpu.VMEM((BLOCKS * COLS, LANES), BF16)],
        compiler_params=params(),
        cost_estimate=cost(2 * ROWS * TOK * D, 2 * (ROWS + TOK) * D),
    )(routes, probs, value)


def noisy_kernel(noise_ref, weight_ref, out_ref):
    row = pl.program_id(0)
    for c in range(weight_ref.shape[1] // 256):
        cut = slice(c * 256, (c + 1) * 256)
        out_ref[:, cut] = (weight_ref[:, cut].astype(F32) * noise_ref[row, c]).astype(BF16)


def noisy(weight, noise):
    height, breadth = weight.shape
    return pl.pallas_call(
        noisy_kernel,
        grid=(height // 256,),
        out_shape=jax.ShapeDtypeStruct(weight.shape, BF16),
        in_specs=[
            pl.BlockSpec(memory_space=pltpu.SMEM),
            pl.BlockSpec((256, breadth), lambda i: (i, 0)),
        ],
        out_specs=pl.BlockSpec((256, breadth), lambda i: (i, 0)),
        compiler_params=params(),
        cost_estimate=cost(height * breadth, 4 * height * breadth),
    )(noise, weight)


def unpack_rows(packed_ref, rows_ref):
    last = unpack_last(packed_ref[:, MAIN * COLS :, :])
    for j in range(COLS):
        cut = slice(j * LANES, (j + 1) * LANES)
        rows_ref[:BIG, cut] = packed_ref[:, j * MAIN : (j + 1) * MAIN, :].reshape(BIG, LANES)
        rows_ref[BIG:, cut] = last[j * BLOCKS : (j + 1) * BLOCKS]


def pack_columns(values, first, out_ref, last_ref):
    for i in range(2):
        cut = values[:, i * LANES : (i + 1) * LANES]
        at = pl.multiple_of((first + i) * MAIN, MAIN)
        out_ref[:, pl.ds(at, MAIN), :] = cut[:BIG].reshape(BLOCKS, MAIN, LANES)
        last_ref[pl.ds(at, BLOCKS), :] = cut[BIG:]


def pack_last(out_ref, last_ref):
    tiles = dot(last_slot_order(False), last_ref[...]).astype(BF16)
    out_ref[:, MAIN * COLS :, :] = tiles.reshape(BLOCKS, COLS, LANES)


def gate_up_kernel(packed_ref, gate_w_ref, up_w_ref, rows_ref, gate_ref, up_ref, hidden_ref):
    @pl.when(pl.program_id(0) == 0)
    def _():
        unpack_rows(packed_ref, rows_ref)

    gate = dot(rows_ref[...], gate_w_ref[...])
    gate_ref[...] = gate
    up = dot(rows_ref[...], up_w_ref[...])
    up_ref[...] = up
    hidden_ref[...] = (gate * jax.nn.sigmoid(gate) * up).astype(BF16)


def gate_up(packed, weight_in):
    wide = FF // 256
    part = pl.BlockSpec((ROWS, 256), lambda i: (0, i))
    return pl.pallas_call(
        gate_up_kernel,
        grid=(wide,),
        out_shape=(
            jax.ShapeDtypeStruct((ROWS, D), BF16),
            jax.ShapeDtypeStruct((ROWS, FF), F32),
            jax.ShapeDtypeStruct((ROWS, FF), F32),
            jax.ShapeDtypeStruct((ROWS, FF), BF16),
        ),
        in_specs=[
            pl.BlockSpec((BLOCKS, PACK, LANES), lambda i: (0, 0, 0)),
            pl.BlockSpec((D, 256), lambda i: (0, i)),
            pl.BlockSpec((D, 256), lambda i: (0, i + wide)),
        ],
        out_specs=(pl.BlockSpec((ROWS, D), lambda i: (0, 0)), part, part, part),
        compiler_params=params(),
        cost_estimate=cost(4 * ROWS * D * FF, 4 * ROWS * D + 4 * D * FF + 10 * ROWS * FF),
    )(packed, weight_in, weight_in)


def down_kernel(hidden_ref, weight_ref, out_ref, last_ref):
    step = pl.program_id(0)
    values = dot(hidden_ref[...], weight_ref[...]).astype(BF16)
    pack_columns(values, step * 2, out_ref, last_ref)

    @pl.when(step == pl.num_programs(0) - 1)
    def _():
        pack_last(out_ref, last_ref)


def down(hidden, weight_out):
    return pl.pallas_call(
        down_kernel,
        grid=(D // 256,),
        out_shape=jax.ShapeDtypeStruct((BLOCKS, PACK, LANES), BF16),
        in_specs=[
            pl.BlockSpec((ROWS, FF), lambda i: (0, 0)),
            pl.BlockSpec((FF, 256), lambda i: (0, i)),
        ],
        out_specs=pl.BlockSpec((BLOCKS, PACK, LANES), lambda i: (0, 0, 0)),
        scratch_shapes=[pltpu.VMEM((BLOCKS * COLS, LANES), BF16)],
        compiler_params=params(),
        cost_estimate=cost(2 * ROWS * D * FF, 2 * ROWS * D + 2 * D * FF + 2 * ROWS * FF),
    )(hidden, weight_out)


def mix_kernel(packed_ref, weight_ref, gate_ref, up_ref, rows_ref, gate_grad_ref, up_grad_ref):
    @pl.when(pl.program_id(0) == 0)
    def _():
        unpack_rows(packed_ref, rows_ref)

    grad = dot_nt(rows_ref[...], weight_ref[...])
    gate = gate_ref[...]
    sigma = jax.nn.sigmoid(gate)
    slope = sigma * (1.0 + gate * (1.0 - sigma))
    gate_grad_ref[...] = (grad * up_ref[...] * slope).astype(BF16)
    up_grad_ref[...] = (grad * gate * sigma).astype(BF16)


def mix(packed, weight_out, gate, up):
    part = pl.BlockSpec((ROWS, 256), lambda i: (0, i))
    return pl.pallas_call(
        mix_kernel,
        grid=(FF // 256,),
        out_shape=(
            jax.ShapeDtypeStruct((ROWS, D), BF16),
            jax.ShapeDtypeStruct((ROWS, FF), BF16),
            jax.ShapeDtypeStruct((ROWS, FF), BF16),
        ),
        in_specs=[
            pl.BlockSpec((BLOCKS, PACK, LANES), lambda i: (0, 0, 0)),
            pl.BlockSpec((256, D), lambda i: (i, 0)),
            part,
            part,
        ],
        out_specs=(pl.BlockSpec((ROWS, D), lambda i: (0, 0)), part, part),
        compiler_params=params(),
        cost_estimate=cost(2 * ROWS * D * FF, 4 * ROWS * D + 2 * D * FF + 12 * ROWS * FF),
    )(packed, weight_out, gate, up)


def input_grad_kernel(gate_grad_ref, up_grad_ref, weight_ref, out_ref, last_ref):
    step = pl.program_id(0)
    values = dot_nt(gate_grad_ref[...], weight_ref[:, :FF])
    values = (values + dot_nt(up_grad_ref[...], weight_ref[:, FF:])).astype(BF16)
    pack_columns(values, step * 2, out_ref, last_ref)

    @pl.when(step == pl.num_programs(0) - 1)
    def _():
        pack_last(out_ref, last_ref)


def input_grads(gate_grad, up_grad, weight_in):
    whole = pl.BlockSpec((ROWS, FF), lambda i: (0, 0))
    return pl.pallas_call(
        input_grad_kernel,
        grid=(D // 256,),
        out_shape=jax.ShapeDtypeStruct((BLOCKS, PACK, LANES), BF16),
        in_specs=[whole, whole, pl.BlockSpec((256, 2 * FF), lambda i: (i, 0))],
        out_specs=pl.BlockSpec((BLOCKS, PACK, LANES), lambda i: (0, 0, 0)),
        scratch_shapes=[pltpu.VMEM((BLOCKS * COLS, LANES), BF16)],
        compiler_params=params(),
        cost_estimate=cost(4 * ROWS * D * FF, 2 * ROWS * D + 4 * D * FF + 4 * ROWS * FF),
    )(gate_grad, up_grad, weight_in)


def weight_in_kernel(share_ref, noise_ref, rows_ref, gate_grad_ref, up_grad_ref, out_ref):
    tile = share_ref[pl.program_id(0)] * 2 + pl.program_id(1)
    for half, grad_ref in enumerate((gate_grad_ref, up_grad_ref)):
        raw = dot_tn(rows_ref[...], grad_ref[...])
        for c in range(FF // 256):
            at = half * FF + c * 256
            scaled = raw[:, c * 256 : (c + 1) * 256] * noise_ref[tile, half * (FF // 256) + c]
            out_ref[0, :, at : at + 256] = scaled.astype(out_ref.dtype)


def weight_in_grads(shares, noise, rows, gate_grad, up_grad, dtype):
    whole = pl.BlockSpec((ROWS, FF), lambda j, i, s: (0, 0))
    return pl.pallas_call(
        weight_in_kernel,
        grid_spec=pltpu.PrefetchScalarGridSpec(
            num_scalar_prefetch=1,
            grid=(2, 2),
            in_specs=[
                pl.BlockSpec(memory_space=pltpu.SMEM),
                pl.BlockSpec((ROWS, 256), lambda j, i, s: (0, s[j] * 2 + i)),
                whole,
                whole,
            ],
            out_specs=pl.BlockSpec((1, 256, 2 * FF), lambda j, i, s: (j, i, 0)),
        ),
        out_shape=jax.ShapeDtypeStruct((2, 512, 2 * FF), dtype),
        compiler_params=params(),
        cost_estimate=cost(2 * ROWS * D * FF, ROWS * D + 4 * ROWS * FF + 4 * D * FF),
    )(shares, noise, rows, gate_grad, up_grad)


def weight_out_kernel(share_ref, noise_ref, hidden_ref, rows_ref, out_ref):
    tile = share_ref[pl.program_id(0)] * 2 + pl.program_id(1)
    raw = dot_tn(hidden_ref[...], rows_ref[...])
    for c in range(FF // 256):
        cut = slice(c * 256, (c + 1) * 256)
        out_ref[0, cut, :] = (raw[cut] * noise_ref[c, tile]).astype(out_ref.dtype)


def weight_out_grads(shares, noise, hidden, rows, dtype):
    return pl.pallas_call(
        weight_out_kernel,
        grid_spec=pltpu.PrefetchScalarGridSpec(
            num_scalar_prefetch=1,
            grid=(2, 2),
            in_specs=[
                pl.BlockSpec(memory_space=pltpu.SMEM),
                pl.BlockSpec((ROWS, FF), lambda j, i, s: (0, 0)),
                pl.BlockSpec((ROWS, 256), lambda j, i, s: (0, s[j] * 2 + i)),
            ],
            out_specs=pl.BlockSpec((1, FF, 256), lambda j, i, s: (j, 0, i)),
        ),
        out_shape=jax.ShapeDtypeStruct((2, FF, 512), dtype),
        compiler_params=params(),
        cost_estimate=cost(ROWS * D * FF, ROWS * D + 2 * ROWS * FF + 2 * D * FF),
    )(shares, noise, hidden, rows)


def combine_tables(routes, weight):
    key = slot_keys(routes)
    spread = jnp.where(iota((LANES, BIG), 1) // MAIN == iota((LANES, BIG), 0), 1.0, 0.0).astype(BF16)
    hit = dot(key.astype(BF16), spread) == (iota((TOK, BIG), 1) % MAIN).astype(F32)
    last_hit = key == float(MAIN)
    if weight is None:
        pick = jnp.where(hit, 1.0, 0.0)
        last_pick = jnp.where(last_hit, 1.0, 0.0)
    else:
        pick = jnp.where(hit, dot(weight.astype(BF16), spread), 0.0)
        last_pick = jnp.where(last_hit, weight, 0.0)
    return key, pick.astype(BF16), last_pick[:, :BLOCKS].astype(BF16)


def combine_kernel(routes_ref, packed_ref, out_ref):
    _, pick, last_pick = combine_tables(routes_ref[...], None)
    last = unpack_last(packed_ref[:, MAIN * COLS :, :])
    for j in range(COLS):
        cut = slice(j * LANES, (j + 1) * LANES)
        rows = packed_ref[:, j * MAIN : (j + 1) * MAIN, :].reshape(BIG, LANES)
        total = dot(pick, rows) + dot(last_pick, last[j * BLOCKS : (j + 1) * BLOCKS])
        out_ref[:, cut] = total.astype(BF16)


def combine(routes, packed):
    return pl.pallas_call(
        combine_kernel,
        out_shape=jax.ShapeDtypeStruct((TOK, D), BF16),
        compiler_params=params(),
        cost_estimate=cost(2 * ROWS * TOK * D, 2 * (ROWS + TOK) * D),
    )(routes, packed)


def combine_output_kernel(routes_ref, probs_ref, cotangent_ref, packed_ref, out_ref, grad_ref, rows_ref):
    routes = routes_ref[...]
    unpack_rows(packed_ref, rows_ref)
    key, pick, last_pick = combine_tables(routes, expert_weights(routes, probs_ref[...]))
    for j in range(D // 256):
        cut = slice(j * 256, (j + 1) * 256)
        total = dot(pick, rows_ref[:BIG, cut]) + dot(last_pick, rows_ref[BIG:, cut])
        out_ref[:, cut] = total.astype(BF16)
    main = dot_nt(cotangent_ref[...], rows_ref[:BIG, :])
    last = dot_nt(cotangent_ref[...], rows_ref[BIG:, :])
    lane = iota((TOK, LANES), 1)
    for k in range(TOP):
        expert = routes[:, k : k + 1]
        slot = jnp.sum(jnp.where(expert == lane, key, 0.0), axis=1, keepdims=True).astype(jnp.int32)
        row = jnp.where(slot < MAIN, expert * MAIN + slot, -1)
        value = jnp.sum(jnp.where(iota((TOK, BIG), 1) == row, main, 0.0), axis=1, keepdims=True)
        row = jnp.where(slot < MAIN, -1, expert)
        value += jnp.sum(jnp.where(iota((TOK, BLOCKS), 1) == row, last, 0.0), axis=1, keepdims=True)
        grad_ref[:, k : k + 1] = value


def combine_output(routes, probs, cotangent, packed):
    return pl.pallas_call(
        combine_output_kernel,
        out_shape=(
            jax.ShapeDtypeStruct((TOK, D), BF16),
            jax.ShapeDtypeStruct((TOK, TOP), F32),
        ),
        scratch_shapes=[pltpu.VMEM((ROWS, D), BF16)],
        compiler_params=params(),
        cost_estimate=cost(4 * ROWS * TOK * D, 2 * (ROWS + 2 * TOK) * D),
    )(routes, probs, cotangent, packed)


def exchange(value):
    return lax.all_to_all(value, "expert", split_axis=0, concat_axis=0, tiled=True)


def across(value, flip):
    pairs = [(s * BLOCKS + e, (s ^ flip) * BLOCKS + e) for s in range(4) for e in range(BLOCKS)]
    return lax.ppermute(value, ("sample", "expert"), pairs)


def shards(tokens, routes, probs, cotangent, w_gate_up, w_down, gu_noise, down_noise):
    routes, probs, cotangent = routes[0], probs[0], cotangent[0]
    gu_noise, down_noise = gu_noise[0, 0], down_noise[0, 0]
    sample = lax.axis_index("sample")
    ours = jnp.stack([sample, sample ^ 2]).astype(jnp.int32)
    theirs = ours ^ 1

    recv_x = exchange(dispatch(routes, probs, tokens[0], False))
    send_dy = dispatch(routes, probs, cotangent, True)
    weight_in = noisy(w_gate_up[0], gu_noise)
    weight_out = noisy(w_down[0], down_noise)
    recv_dy = exchange(send_dy)
    rows_x, gate, up, hidden = gate_up(recv_x, weight_in)
    output = down(hidden, weight_out)
    back_y = exchange(output)
    rows_dy, gate_grad, up_grad = mix(recv_dy, weight_out, gate, up)

    sent_in = weight_in_grads(theirs, gu_noise, rows_x, gate_grad, up_grad, BF16)
    got_in = across(sent_in, 1)
    sent_out = weight_out_grads(theirs, down_noise, hidden, rows_dy, BF16)
    got_out = across(sent_out, 1)
    kept_in = weight_in_grads(ours, gu_noise, rows_x, gate_grad, up_grad, F32)
    kept_out = weight_out_grads(ours, down_noise, hidden, rows_dy, F32)
    far_in = across((kept_in[1] + got_in[1].astype(F32)).astype(BF16), 2)
    far_out = across((kept_out[1] + got_out[1].astype(F32)).astype(BF16), 2)
    back_dx = exchange(input_grads(gate_grad, up_grad, weight_in))

    layer_out, prob_grad = combine_output(routes, probs, cotangent, back_y)
    input_grad = combine(routes, back_dx)
    grad_in = (kept_in[0] + got_in[0].astype(F32) + far_in.astype(F32)) * 0.25
    grad_out = (kept_out[0] + got_out[0].astype(F32) + far_out.astype(F32)) * 0.25
    return (layer_out[None], input_grad[None], prob_grad[None], grad_in[None], grad_out[None])


def solution(mesh):
    tokens = P("sample", "expert", None)
    noise = P("sample", "expert", None, None)
    experts = P("expert", None, None)
    in_specs = (tokens, tokens, tokens, tokens, experts, experts, noise, noise)
    out_specs = (tokens, tokens, tokens, P("expert", "sample", None), P("expert", None, "sample"))
    return jax.shard_map(shards, mesh=mesh, in_specs=in_specs, out_specs=out_specs, check_vma=False)
```

```python
import functools

import jax
import jax.numpy as jnp
from jax import lax
from jax.experimental import pallas as pl
from jax.experimental.pallas import tpu as pltpu
from jax.sharding import PartitionSpec as P

D = 2048
FF = 768
TOP = 8
TOK = 128
BLOCKS = 32
LANES = 128
COLS = D // LANES
MAIN = 32
PACK = MAIN * COLS + COLS
ROWS = BLOCKS * (MAIN + 1)
BIG = BLOCKS * MAIN
VMEM_LIMIT = 48 * 1024 * 1024

F32 = jnp.float32
BF16 = jnp.bfloat16


def params(**more):
    return pltpu.CompilerParams(vmem_limit_bytes=VMEM_LIMIT, **more)


def cost(flops, moved):
    return pl.CostEstimate(flops=flops // 1000, bytes_accessed=moved // 1000, transcendentals=0)


def iota(shape, dim):
    return lax.broadcasted_iota(jnp.int32, shape, dim)


def dot(a, b):
    return jnp.dot(a, b, preferred_element_type=F32)


def dot_nt(a, b):
    return lax.dot_general(a, b, (((1,), (1,)), ((), ())), preferred_element_type=F32)


def dot_tn(a, b):
    return lax.dot_general(a, b, (((0,), (0,)), ((), ())), preferred_element_type=F32)


AFTER = pl.BlockSpec(memory_space=pl.ANY)


def slot_keys(routes):
    expert = iota((LANES, TOK), 0)
    chosen = jnp.zeros((LANES, TOK), F32)
    for k in range(TOP):
        chosen = jnp.where(routes[k : k + 1, :] == expert, 1.0, chosen)
    earlier = jnp.where(iota((TOK, TOK), 0) < iota((TOK, TOK), 1), 1.0, 0.0).astype(BF16)
    rank = dot(chosen.astype(BF16), earlier)
    return jnp.where(chosen > 0.0, rank, -1.0)


def expert_weights(routes, probs):
    expert = iota((LANES, TOK), 0)
    weight = jnp.zeros((LANES, TOK), F32)
    for k in range(TOP):
        weight = jnp.where(routes[k : k + 1, :] == expert, probs[k : k + 1, :].astype(F32), weight)
    return weight


def last_slot_order(receive):
    count = BLOCKS * COLS
    tile = iota((count, count), 1 if receive else 0)
    row = iota((count, count), 0 if receive else 1)
    same = ((tile // COLS) == (row % BLOCKS)) & ((tile % COLS) == (row // BLOCKS))
    return jnp.where(same, 1.0, 0.0).astype(BF16)


def unpack_last(tile):
    flat = tile.reshape(BLOCKS * COLS, LANES)
    return dot(last_slot_order(True), flat).astype(BF16)


def dispatch_kernel(
    routes_ref, probs_ref, tokens_ref, cotangent_ref, after_ref, x_ref, dy_ref, last_x_ref, last_dy_ref
):
    routes = routes_ref[...]
    key = slot_keys(routes)
    weight = expert_weights(routes, probs_ref[...])
    spread = jnp.where(iota((BIG, LANES), 0) // MAIN == iota((BIG, LANES), 1), 1.0, 0.0).astype(BF16)
    hit = dot(spread, key.astype(BF16)) == (iota((BIG, TOK), 0) % MAIN).astype(F32)
    last_hit = key[:BLOCKS] == float(MAIN)
    order = last_slot_order(False)

    def send(value_ref, pick, last_pick, out_ref, last_ref):
        for j in range(COLS):
            value = value_ref[:, j * LANES : (j + 1) * LANES]
            rows = dot(pick, value).astype(BF16)
            out_ref[:, j * MAIN : (j + 1) * MAIN, :] = rows.reshape(BLOCKS, MAIN, LANES)
            last_ref[j * BLOCKS : (j + 1) * BLOCKS, :] = dot(last_pick, value).astype(BF16)
        tiles = dot(order, last_ref[...]).astype(BF16)
        out_ref[:, MAIN * COLS :, :] = tiles.reshape(BLOCKS, COLS, LANES)

    pick = jnp.where(hit, 1.0, 0.0).astype(BF16)
    last_pick = jnp.where(last_hit, 1.0, 0.0).astype(BF16)
    send(tokens_ref, pick, last_pick, x_ref, last_x_ref)
    pick = jnp.where(hit, dot(spread, weight.astype(BF16)), 0.0).astype(BF16)
    last_pick = jnp.where(last_hit, weight[:BLOCKS], 0.0).astype(BF16)
    send(cotangent_ref, pick, last_pick, dy_ref, last_dy_ref)


def dispatch(routes, probs, tokens, cotangent, after):
    packed = jax.ShapeDtypeStruct((BLOCKS, PACK, LANES), BF16)
    return pl.pallas_call(
        dispatch_kernel,
        out_shape=(packed, packed),
        in_specs=[pl.BlockSpec(memory_space=pltpu.VMEM)] * 4 + [AFTER],
        scratch_shapes=[pltpu.VMEM((BLOCKS * COLS, LANES), BF16)] * 2,
        compiler_params=params(),
        cost_estimate=cost(4 * ROWS * TOK * D, 4 * (ROWS + TOK) * D),
    )(routes, probs, tokens, cotangent, after)


def noisy_kernel(noise_ref, weight_ref, after_ref, out_ref):
    row = pl.program_id(0)
    for c in range(weight_ref.shape[1] // 256):
        cut = slice(c * 256, (c + 1) * 256)
        out_ref[:, cut] = (weight_ref[:, cut].astype(F32) * noise_ref[row, c]).astype(BF16)


def noisy(weight, noise, after):
    height, breadth = weight.shape
    return pl.pallas_call(
        noisy_kernel,
        grid=(height // 256,),
        out_shape=jax.ShapeDtypeStruct(weight.shape, BF16),
        in_specs=[
            pl.BlockSpec(memory_space=pltpu.SMEM),
            pl.BlockSpec((256, breadth), lambda i: (i, 0)),
            AFTER,
        ],
        out_specs=pl.BlockSpec((256, breadth), lambda i: (i, 0)),
        compiler_params=params(),
        cost_estimate=cost(height * breadth, 4 * height * breadth),
    )(noise, weight, after)


def unpack_rows(packed_ref, rows_ref):
    last = unpack_last(packed_ref[:, MAIN * COLS :, :])
    for j in range(COLS):
        cut = slice(j * LANES, (j + 1) * LANES)
        rows_ref[:BIG, cut] = packed_ref[:, j * MAIN : (j + 1) * MAIN, :].reshape(BIG, LANES)
        rows_ref[BIG:, cut] = last[j * BLOCKS : (j + 1) * BLOCKS]


def pack_columns(values, first, out_ref, last_ref):
    for i in range(2):
        cut = values[:, i * LANES : (i + 1) * LANES]
        at = pl.multiple_of((first + i) * MAIN, MAIN)
        out_ref[:, pl.ds(at, MAIN), :] = cut[:BIG].reshape(BLOCKS, MAIN, LANES)
        last_ref[pl.ds(at, BLOCKS), :] = cut[BIG:]


def pack_last(out_ref, last_ref):
    tiles = dot(last_slot_order(False), last_ref[...]).astype(BF16)
    out_ref[:, MAIN * COLS :, :] = tiles.reshape(BLOCKS, COLS, LANES)


def gate_up_kernel(packed_ref, gate_w_ref, up_w_ref, rows_ref, gate_ref, up_ref, hidden_ref):
    @pl.when(pl.program_id(0) == 0)
    def _():
        unpack_rows(packed_ref, rows_ref)

    gate = dot(rows_ref[...], gate_w_ref[...])
    gate_ref[...] = gate
    up = dot(rows_ref[...], up_w_ref[...])
    up_ref[...] = up
    hidden_ref[...] = (gate * jax.nn.sigmoid(gate) * up).astype(BF16)


def gate_up(packed, weight_in):
    wide = FF // 256
    part = pl.BlockSpec((ROWS, 256), lambda i: (0, i))
    return pl.pallas_call(
        gate_up_kernel,
        grid=(wide,),
        out_shape=(
            jax.ShapeDtypeStruct((ROWS, D), BF16),
            jax.ShapeDtypeStruct((ROWS, FF), F32),
            jax.ShapeDtypeStruct((ROWS, FF), F32),
            jax.ShapeDtypeStruct((ROWS, FF), BF16),
        ),
        in_specs=[
            pl.BlockSpec((BLOCKS, PACK, LANES), lambda i: (0, 0, 0)),
            pl.BlockSpec((D, 256), lambda i: (0, i)),
            pl.BlockSpec((D, 256), lambda i: (0, i + wide)),
        ],
        out_specs=(pl.BlockSpec((ROWS, D), lambda i: (0, 0)), part, part, part),
        compiler_params=params(),
        cost_estimate=cost(4 * ROWS * D * FF, 4 * ROWS * D + 4 * D * FF + 10 * ROWS * FF),
    )(packed, weight_in, weight_in)


def down_kernel(hidden_ref, weight_ref, out_ref, last_ref):
    step = pl.program_id(0)
    values = dot(hidden_ref[...], weight_ref[...]).astype(BF16)
    pack_columns(values, step * 2, out_ref, last_ref)

    @pl.when(step == pl.num_programs(0) - 1)
    def _():
        pack_last(out_ref, last_ref)


def down(hidden, weight_out):
    return pl.pallas_call(
        down_kernel,
        grid=(D // 256,),
        out_shape=jax.ShapeDtypeStruct((BLOCKS, PACK, LANES), BF16),
        in_specs=[
            pl.BlockSpec((ROWS, FF), lambda i: (0, 0)),
            pl.BlockSpec((FF, 256), lambda i: (0, i)),
        ],
        out_specs=pl.BlockSpec((BLOCKS, PACK, LANES), lambda i: (0, 0, 0)),
        scratch_shapes=[pltpu.VMEM((BLOCKS * COLS, LANES), BF16)],
        compiler_params=params(),
        cost_estimate=cost(2 * ROWS * D * FF, 2 * ROWS * D + 2 * D * FF + 2 * ROWS * FF),
    )(hidden, weight_out)


def mix_kernel(packed_ref, weight_ref, gate_ref, up_ref, after_ref, rows_ref, gate_grad_ref, up_grad_ref):
    @pl.when(pl.program_id(0) == 0)
    def _():
        unpack_rows(packed_ref, rows_ref)

    grad = dot_nt(rows_ref[...], weight_ref[...])
    gate = gate_ref[...]
    sigma = jax.nn.sigmoid(gate)
    slope = sigma * (1.0 + gate * (1.0 - sigma))
    gate_grad_ref[...] = (grad * up_ref[...] * slope).astype(BF16)
    up_grad_ref[...] = (grad * gate * sigma).astype(BF16)


def mix(packed, weight_out, gate, up, after):
    part = pl.BlockSpec((ROWS, 256), lambda i: (0, i))
    return pl.pallas_call(
        mix_kernel,
        grid=(FF // 256,),
        out_shape=(
            jax.ShapeDtypeStruct((ROWS, D), BF16),
            jax.ShapeDtypeStruct((ROWS, FF), BF16),
            jax.ShapeDtypeStruct((ROWS, FF), BF16),
        ),
        in_specs=[
            pl.BlockSpec((BLOCKS, PACK, LANES), lambda i: (0, 0, 0)),
            pl.BlockSpec((256, D), lambda i: (i, 0)),
            part,
            part,
            AFTER,
        ],
        out_specs=(pl.BlockSpec((ROWS, D), lambda i: (0, 0)), part, part),
        compiler_params=params(),
        cost_estimate=cost(2 * ROWS * D * FF, 4 * ROWS * D + 2 * D * FF + 12 * ROWS * FF),
    )(packed, weight_out, gate, up, after)


def input_grad_kernel(gate_grad_ref, up_grad_ref, weight_ref, after_in, after_out, out_ref, last_ref):
    step = pl.program_id(0)
    values = dot_nt(gate_grad_ref[...], weight_ref[:, :FF])
    values = (values + dot_nt(up_grad_ref[...], weight_ref[:, FF:])).astype(BF16)
    pack_columns(values, step * 2, out_ref, last_ref)

    @pl.when(step == pl.num_programs(0) - 1)
    def _():
        pack_last(out_ref, last_ref)


def input_grads(gate_grad, up_grad, weight_in, after):
    whole = pl.BlockSpec((ROWS, FF), lambda i: (0, 0))
    return pl.pallas_call(
        input_grad_kernel,
        grid=(D // 256,),
        out_shape=jax.ShapeDtypeStruct((BLOCKS, PACK, LANES), BF16),
        in_specs=[whole, whole, pl.BlockSpec((256, 2 * FF), lambda i: (i, 0)), AFTER, AFTER],
        out_specs=pl.BlockSpec((BLOCKS, PACK, LANES), lambda i: (0, 0, 0)),
        scratch_shapes=[pltpu.VMEM((BLOCKS * COLS, LANES), BF16)],
        compiler_params=params(),
        cost_estimate=cost(4 * ROWS * D * FF, 2 * ROWS * D + 4 * D * FF + 4 * ROWS * FF),
    )(gate_grad, up_grad, weight_in, *after)


def weight_in_kernel(share_ref, noise_ref, rows_ref, gate_grad_ref, up_grad_ref, after_ref, out_ref):
    tile = share_ref[pl.program_id(0)] * 2 + pl.program_id(1)
    for half, grad_ref in enumerate((gate_grad_ref, up_grad_ref)):
        raw = dot_tn(rows_ref[...], grad_ref[...])
        for c in range(FF // 256):
            at = half * FF + c * 256
            scaled = raw[:, c * 256 : (c + 1) * 256] * noise_ref[tile, half * (FF // 256) + c]
            out_ref[0, :, at : at + 256] = scaled.astype(out_ref.dtype)


def weight_in_grads(shares, noise, rows, gate_grad, up_grad, dtype, after):
    whole = pl.BlockSpec((ROWS, FF), lambda j, i, s: (0, 0))
    return pl.pallas_call(
        weight_in_kernel,
        grid_spec=pltpu.PrefetchScalarGridSpec(
            num_scalar_prefetch=1,
            grid=(2, 2),
            in_specs=[
                pl.BlockSpec(memory_space=pltpu.SMEM),
                pl.BlockSpec((ROWS, 256), lambda j, i, s: (0, s[j] * 2 + i)),
                whole,
                whole,
                AFTER,
            ],
            out_specs=pl.BlockSpec((1, 256, 2 * FF), lambda j, i, s: (j, i, 0)),
        ),
        out_shape=jax.ShapeDtypeStruct((2, 512, 2 * FF), dtype),
        compiler_params=params(),
        cost_estimate=cost(2 * ROWS * D * FF, ROWS * D + 4 * ROWS * FF + 4 * D * FF),
    )(shares, noise, rows, gate_grad, up_grad, after)


def weight_out_kernel(share_ref, noise_ref, hidden_ref, rows_ref, out_ref):
    tile = share_ref[pl.program_id(0)] * 2 + pl.program_id(1)
    raw = dot_tn(hidden_ref[...], rows_ref[...])
    for c in range(FF // 256):
        cut = slice(c * 256, (c + 1) * 256)
        out_ref[0, cut, :] = (raw[cut] * noise_ref[c, tile]).astype(out_ref.dtype)


def weight_out_grads(shares, noise, hidden, rows, dtype):
    return pl.pallas_call(
        weight_out_kernel,
        grid_spec=pltpu.PrefetchScalarGridSpec(
            num_scalar_prefetch=1,
            grid=(2, 2),
            in_specs=[
                pl.BlockSpec(memory_space=pltpu.SMEM),
                pl.BlockSpec((ROWS, FF), lambda j, i, s: (0, 0)),
                pl.BlockSpec((ROWS, 256), lambda j, i, s: (0, s[j] * 2 + i)),
            ],
            out_specs=pl.BlockSpec((1, FF, 256), lambda j, i, s: (j, 0, i)),
        ),
        out_shape=jax.ShapeDtypeStruct((2, FF, 512), dtype),
        compiler_params=params(),
        cost_estimate=cost(ROWS * D * FF, ROWS * D + 2 * ROWS * FF + 2 * D * FF),
    )(shares, noise, hidden, rows)


def combine_tables(key, weight):
    key = key.T
    spread = jnp.where(iota((LANES, BIG), 1) // MAIN == iota((LANES, BIG), 0), 1.0, 0.0).astype(BF16)
    hit = dot(key.astype(BF16), spread) == (iota((TOK, BIG), 1) % MAIN).astype(F32)
    last_hit = key == float(MAIN)
    if weight is None:
        pick = jnp.where(hit, 1.0, 0.0)
        last_pick = jnp.where(last_hit, 1.0, 0.0)
    else:
        weight = weight.T
        pick = jnp.where(hit, dot(weight.astype(BF16), spread), 0.0)
        last_pick = jnp.where(last_hit, weight, 0.0)
    return pick.astype(BF16), last_pick[:, :BLOCKS].astype(BF16)


def combine_kernel(place_ref, routes_ref, packed_ref, *refs):
    out_ref = refs[-1]
    experts = BLOCKS // 2
    key = slot_keys(routes_ref[...]).T + 1.0
    plane = place_ref[1]

    def spread(shape, width):
        return jnp.where(iota(shape, 0) == iota(shape, 1) // width * 2 + plane, 1.0, 0.0).astype(BF16)

    main = (TOK, experts * MAIN)
    hit = dot(key.astype(BF16), spread((LANES, experts * MAIN), MAIN))
    pick = jnp.where(hit == (iota(main, 1) % MAIN + 1).astype(F32), 1.0, 0.0).astype(BF16)
    hit = dot(key.astype(BF16), spread((LANES, LANES), 1))
    last_pick = jnp.where(hit == float(MAIN + 1), 1.0, 0.0).astype(BF16)[:, :experts]

    count = experts * COLS
    row, tile = iota((count, count), 0), iota((count, count), 1)
    order = ((tile // COLS) == (row % experts)) & ((tile % COLS) == (row // experts))
    last = packed_ref[:, 0, MAIN * COLS :, :].reshape(count, LANES)
    last = dot(jnp.where(order, 1.0, 0.0).astype(BF16), last).astype(BF16)
    for j in range(COLS):
        rows = packed_ref[:, 0, j * MAIN : (j + 1) * MAIN, :].reshape(experts * MAIN, LANES)
        total = dot(pick, rows) + dot(last_pick, last[j * experts : (j + 1) * experts])
        out_ref[:, j * LANES : (j + 1) * LANES] = total.astype(out_ref.dtype)


def combine(place, routes, packed, dtype, after):
    experts = BLOCKS // 2
    return pl.pallas_call(
        combine_kernel,
        grid_spec=pltpu.PrefetchScalarGridSpec(
            num_scalar_prefetch=1,
            grid=(1,),
            in_specs=[
                pl.BlockSpec((TOP, TOK), lambda i, p: (0, 0)),
                pl.BlockSpec((experts, 1, PACK, LANES), lambda i, p: (0, p[0], 0, 0)),
                *[AFTER] * len(after),
            ],
            out_specs=pl.BlockSpec((TOK, D), lambda i, p: (0, 0)),
        ),
        out_shape=jax.ShapeDtypeStruct((TOK, D), dtype),
        compiler_params=params(),
        cost_estimate=cost(ROWS * TOK * D, (ROWS + 2 * TOK) * D),
    )(place, routes, packed.reshape(experts, 2, PACK, LANES), *after)


def finish_kernel(kept_ref, got_ref, far_ref, after_ref, out_ref):
    total = kept_ref[0] + got_ref[0].astype(F32) + far_ref[...].astype(F32)
    out_ref[...] = total * 0.25


def finish(kept, got, far, after):
    height, breadth = far.shape
    first = pl.BlockSpec((1, 128, breadth), lambda i: (0, i, 0))
    part = pl.BlockSpec((128, breadth), lambda i: (i, 0))
    return pl.pallas_call(
        finish_kernel,
        grid=(height // 128,),
        out_shape=jax.ShapeDtypeStruct((height, breadth), F32),
        in_specs=[first, first, part, AFTER],
        out_specs=part,
        compiler_params=params(),
        cost_estimate=cost(3 * height * breadth, 12 * height * breadth),
    )(kept, got, far, after)


def combine_output_kernel(routes_ref, probs_ref, cotangent_ref, packed_ref, out_ref, grad_ref, rows_ref):
    routes = routes_ref[...]
    unpack_rows(packed_ref, rows_ref)
    key = slot_keys(routes)
    pick, last_pick = combine_tables(key, expert_weights(routes, probs_ref[...]))
    for j in range(D // 256):
        cut = slice(j * 256, (j + 1) * 256)
        total = dot(pick, rows_ref[:BIG, cut]) + dot(last_pick, rows_ref[BIG:, cut])
        out_ref[:, cut] = total.astype(BF16)
    main = dot_nt(rows_ref[:BIG, :], cotangent_ref[...])
    last = dot_nt(rows_ref[BIG:, :], cotangent_ref[...])
    for k in range(TOP):
        expert = routes[k : k + 1, :]
        slot = jnp.sum(jnp.where(expert == iota((LANES, TOK), 0), key, 0.0), axis=0, keepdims=True)
        slot = slot.astype(jnp.int32)
        row = jnp.where(slot < MAIN, expert * MAIN + slot, -1)
        value = jnp.sum(jnp.where(iota((BIG, TOK), 0) == row, main, 0.0), axis=0, keepdims=True)
        row = jnp.where(slot < MAIN, -1, expert)
        value += jnp.sum(jnp.where(iota((BLOCKS, TOK), 0) == row, last, 0.0), axis=0, keepdims=True)
        grad_ref[k : k + 1, :] = value


def combine_output(routes, probs, cotangent, packed):
    return pl.pallas_call(
        combine_output_kernel,
        out_shape=(
            jax.ShapeDtypeStruct((TOK, D), BF16),
            jax.ShapeDtypeStruct((TOP, TOK), F32),
        ),
        scratch_shapes=[pltpu.VMEM((ROWS, D), BF16)],
        compiler_params=params(),
        cost_estimate=cost(4 * ROWS * TOK * D, 2 * (ROWS + 2 * TOK) * D),
    )(routes, probs, cotangent, packed)


def exchange(value):
    return lax.all_to_all(value, "expert", split_axis=0, concat_axis=0, tiled=True)


def exchange_in_plane(value):
    planes = [list(range(z, BLOCKS, 2)) for z in range(2)]
    value = value.reshape(BLOCKS // 2, 2 * PACK, LANES)
    return lax.all_to_all(
        value, "expert", split_axis=0, concat_axis=0, tiled=True, axis_index_groups=planes
    )


def between_planes(value):
    return lax.ppermute(value, "expert", [(e, e ^ 1) for e in range(BLOCKS)])


def across(value, flip):
    pairs = [(s * BLOCKS + e, (s ^ flip) * BLOCKS + e) for s in range(4) for e in range(BLOCKS)]
    return lax.ppermute(value, ("sample", "expert"), pairs)


def shards(tokens, routes, probs, cotangent, w_gate_up, w_down, gu_noise, down_noise):
    routes, probs, cotangent = routes[0].T, probs[0].T, cotangent[0]
    gu_noise, down_noise = gu_noise[0, 0], down_noise[0, 0]
    sample = lax.axis_index("sample")
    ours = jnp.stack([sample, sample ^ 2]).astype(jnp.int32)
    theirs = ours ^ 1

    far_routes = between_planes(routes)
    send_x, send_dy = dispatch(routes, probs, tokens[0], cotangent, far_routes)
    recv_x = exchange(send_x)
    weight_in = noisy(w_gate_up[0], gu_noise, recv_x)
    weight_out = noisy(w_down[0], down_noise, recv_x)
    recv_dy = exchange(send_dy)
    rows_x, gate, up, hidden = gate_up(recv_x, weight_in)
    output = down(hidden, weight_out)
    back_y = exchange(output)
    rows_dy, gate_grad, up_grad = mix(recv_dy, weight_out, gate, up, output)

    sent_in = weight_in_grads(theirs, gu_noise, rows_x, gate_grad, up_grad, BF16, output)
    got_in = across(sent_in, 1)
    sent_out = weight_out_grads(theirs, down_noise, hidden, rows_dy, BF16)
    got_out = across(sent_out, 1)
    kept_in = weight_in_grads(ours, gu_noise, rows_x, gate_grad, up_grad, F32, output)
    kept_out = weight_out_grads(ours, down_noise, hidden, rows_dy, F32)
    half_in = (kept_in[1] + got_in[1].astype(F32)).astype(BF16)
    half_out = (kept_out[1] + got_out[1].astype(F32)).astype(BF16)
    far_in = across(half_in, 2)
    far_out = across(half_out, 2)
    send_dx = input_grads(gate_grad, up_grad, weight_in, (half_in, half_out))
    back_dx = exchange_in_plane(send_dx)

    layer_out, prob_grad = combine_output(routes, probs, cotangent, back_y)
    plane = lax.axis_index("expert") % 2
    place = jnp.stack([1 - plane, plane]).astype(jnp.int32)
    there = combine(place, far_routes, back_dx, BF16, (layer_out,))
    place = jnp.stack([plane, plane]).astype(jnp.int32)
    here = combine(place, routes, back_dx, F32, (there,))
    grad_in = finish(kept_in, got_in, far_in, there)
    grad_out = finish(kept_out, got_out, far_out, there)
    input_grad = (here + between_planes(there).astype(F32)).astype(BF16)
    return (layer_out[None], input_grad[None], prob_grad.T[None], grad_in[None], grad_out[None])


def solution(mesh):
    tokens = P("sample", "expert", None)
    noise = P("sample", "expert", None, None)
    experts = P("expert", None, None)
    in_specs = (tokens, tokens, tokens, tokens, experts, experts, noise, noise)
    out_specs = (tokens, tokens, tokens, P("expert", "sample", None), P("expert", None, "sample"))
    return jax.shard_map(shards, mesh=mesh, in_specs=in_specs, out_specs=out_specs, check_vma=False)
```

```python
import functools

import jax
import jax.numpy as jnp
from jax import lax
from jax.experimental import pallas as pl
from jax.experimental.pallas import tpu as pltpu
from jax.sharding import PartitionSpec as P

D = 2048
FF = 768
TOP = 8
TOK = 128
BLOCKS = 32
LANES = 128
COLS = D // LANES
MAIN = 32
PACK = MAIN * COLS + COLS
ROWS = BLOCKS * (MAIN + 1)
BIG = BLOCKS * MAIN
VMEM_LIMIT = 48 * 1024 * 1024

F32 = jnp.float32
BF16 = jnp.bfloat16


def params(limit=VMEM_LIMIT):
    return pltpu.CompilerParams(vmem_limit_bytes=limit)


def cost(flops, moved):
    return pl.CostEstimate(flops=flops // 1000, bytes_accessed=moved // 1000, transcendentals=0)


def iota(shape, dim):
    return lax.broadcasted_iota(jnp.int32, shape, dim)


def dot(a, b):
    return jnp.dot(a, b, preferred_element_type=F32)


def dot_nt(a, b):
    return lax.dot_general(a, b, (((1,), (1,)), ((), ())), preferred_element_type=F32)


def dot_tn(a, b):
    return lax.dot_general(a, b, (((0,), (0,)), ((), ())), preferred_element_type=F32)


STAYS = pl.BlockSpec(memory_space=pl.ANY)


def slot_keys(routes):
    expert = iota((LANES, TOK), 0)
    chosen = jnp.zeros((LANES, TOK), F32)
    for k in range(TOP):
        chosen = jnp.where(routes[k : k + 1, :] == expert, 1.0, chosen)
    earlier = jnp.where(iota((TOK, TOK), 0) < iota((TOK, TOK), 1), 1.0, 0.0).astype(BF16)
    rank = dot(chosen.astype(BF16), earlier)
    return jnp.where(chosen > 0.0, rank, -1.0)


def expert_weights(routes, probs):
    expert = iota((LANES, TOK), 0)
    weight = jnp.zeros((LANES, TOK), F32)
    for k in range(TOP):
        weight = jnp.where(routes[k : k + 1, :] == expert, probs[k : k + 1, :].astype(F32), weight)
    return weight


def last_slot_order(receive):
    count = BLOCKS * COLS
    tile = iota((count, count), 1 if receive else 0)
    row = iota((count, count), 0 if receive else 1)
    same = ((tile // COLS) == (row % BLOCKS)) & ((tile % COLS) == (row // BLOCKS))
    return jnp.where(same, 1.0, 0.0).astype(BF16)


def unpack_last(tile):
    flat = tile.reshape(BLOCKS * COLS, LANES)
    return dot(last_slot_order(True), flat).astype(BF16)


def dispatch_kernel(
    routes_ref, probs_ref, tokens_hbm, cotangent_hbm, x_hbm, dy_hbm,
    tokens_ref, cotangent_ref, x_ref, dy_ref, last_ref, load_sem, store_sem,
):
    loads = [
        pltpu.make_async_copy(tokens_hbm, tokens_ref, load_sem.at[0]),
        pltpu.make_async_copy(cotangent_hbm, cotangent_ref, load_sem.at[1]),
    ]
    stores = [
        pltpu.make_async_copy(x_ref, x_hbm, store_sem.at[0]),
        pltpu.make_async_copy(dy_ref, dy_hbm, store_sem.at[1]),
    ]
    for load in loads:
        load.start()
    routes = routes_ref[...]
    key = slot_keys(routes)
    weight = expert_weights(routes, probs_ref[...])
    spread = jnp.where(iota((BIG, LANES), 0) // MAIN == iota((BIG, LANES), 1), 1.0, 0.0).astype(BF16)
    hit = dot(spread, key.astype(BF16)) == (iota((BIG, TOK), 0) % MAIN).astype(F32)
    last_hit = key[:BLOCKS] == float(MAIN)
    order = last_slot_order(False)

    def fill(value_ref, pick, last_pick, out_ref):
        for j in range(COLS):
            value = value_ref[:, j * LANES : (j + 1) * LANES]
            rows = dot(pick, value).astype(BF16)
            out_ref[:, j * MAIN : (j + 1) * MAIN, :] = rows.reshape(BLOCKS, MAIN, LANES)
            last_ref[j * BLOCKS : (j + 1) * BLOCKS, :] = dot(last_pick, value).astype(BF16)
        tiles = dot(order, last_ref[...]).astype(BF16)
        out_ref[:, MAIN * COLS :, :] = tiles.reshape(BLOCKS, COLS, LANES)

    pick = jnp.where(hit, 1.0, 0.0).astype(BF16)
    last_pick = jnp.where(last_hit, 1.0, 0.0).astype(BF16)
    loads[0].wait()
    fill(tokens_ref, pick, last_pick, x_ref)
    stores[0].start()
    pick = jnp.where(hit, dot(spread, weight.astype(BF16)), 0.0).astype(BF16)
    last_pick = jnp.where(last_hit, weight[:BLOCKS], 0.0).astype(BF16)
    loads[1].wait()
    fill(cotangent_ref, pick, last_pick, dy_ref)
    stores[1].start()
    for store in stores:
        store.wait()


def dispatch(routes, probs, tokens, cotangent):
    packed = jax.ShapeDtypeStruct((BLOCKS, PACK, LANES), BF16)
    choice = pl.BlockSpec((TOP, TOK), lambda i: (0, 0))
    return pl.pallas_call(
        dispatch_kernel,
        grid=(1,),
        out_shape=(packed, packed),
        in_specs=[choice, choice, STAYS, STAYS],
        out_specs=(STAYS, STAYS),
        scratch_shapes=[
            pltpu.VMEM((TOK, D), BF16),
            pltpu.VMEM((TOK, D), BF16),
            pltpu.VMEM((BLOCKS, PACK, LANES), BF16),
            pltpu.VMEM((BLOCKS, PACK, LANES), BF16),
            pltpu.VMEM((BLOCKS * COLS, LANES), BF16),
            pltpu.SemaphoreType.DMA((2,)),
            pltpu.SemaphoreType.DMA((2,)),
        ],
        compiler_params=params(60 * 1024 * 1024),
        cost_estimate=cost(4 * ROWS * TOK * D, 4 * (ROWS + TOK) * D),
    )(routes, probs, tokens, cotangent)


def noisy_kernel(noise_ref, weight_ref, after_ref, out_ref):
    row = pl.program_id(0)
    for c in range(weight_ref.shape[1] // 256):
        cut = slice(c * 256, (c + 1) * 256)
        out_ref[:, cut] = (weight_ref[:, cut].astype(F32) * noise_ref[row, c]).astype(BF16)


def noisy(weight, noise, after):
    height, breadth = weight.shape
    return pl.pallas_call(
        noisy_kernel,
        grid=(height // 256,),
        out_shape=jax.ShapeDtypeStruct(weight.shape, BF16),
        in_specs=[
            pl.BlockSpec(memory_space=pltpu.SMEM),
            pl.BlockSpec((256, breadth), lambda i: (i, 0)),
            STAYS,
        ],
        out_specs=pl.BlockSpec((256, breadth), lambda i: (i, 0)),
        compiler_params=params(),
        cost_estimate=cost(height * breadth, 4 * height * breadth),
    )(noise, weight, after)


def unpack_rows(packed_ref, rows_ref):
    last = unpack_last(packed_ref[:, MAIN * COLS :, :])
    for j in range(COLS):
        cut = slice(j * LANES, (j + 1) * LANES)
        rows_ref[:BIG, cut] = packed_ref[:, j * MAIN : (j + 1) * MAIN, :].reshape(BIG, LANES)
        rows_ref[BIG:, cut] = last[j * BLOCKS : (j + 1) * BLOCKS]


def pack_columns(values, first, out_ref, last_ref):
    for i in range(2):
        cut = values[:, i * LANES : (i + 1) * LANES]
        at = pl.multiple_of((first + i) * MAIN, MAIN)
        out_ref[:, pl.ds(at, MAIN), :] = cut[:BIG].reshape(BLOCKS, MAIN, LANES)
        last_ref[pl.ds(at, BLOCKS), :] = cut[BIG:]


def pack_last(out_ref, last_ref):
    tiles = dot(last_slot_order(False), last_ref[...]).astype(BF16)
    out_ref[:, MAIN * COLS :, :] = tiles.reshape(BLOCKS, COLS, LANES)


def gate_up_kernel(packed_ref, gate_w_ref, up_w_ref, rows_ref, gate_ref, up_ref, hidden_ref):
    @pl.when(pl.program_id(0) == 0)
    def _():
        unpack_rows(packed_ref, rows_ref)

    gate = dot(rows_ref[...], gate_w_ref[...])
    gate_ref[...] = gate
    up = dot(rows_ref[...], up_w_ref[...])
    up_ref[...] = up
    hidden_ref[...] = (gate * jax.nn.sigmoid(gate) * up).astype(BF16)


def gate_up(packed, weight_in):
    wide = FF // 256
    part = pl.BlockSpec((ROWS, 256), lambda i: (0, i))
    return pl.pallas_call(
        gate_up_kernel,
        grid=(wide,),
        out_shape=(
            jax.ShapeDtypeStruct((ROWS, D), BF16),
            jax.ShapeDtypeStruct((ROWS, FF), F32),
            jax.ShapeDtypeStruct((ROWS, FF), F32),
            jax.ShapeDtypeStruct((ROWS, FF), BF16),
        ),
        in_specs=[
            pl.BlockSpec((BLOCKS, PACK, LANES), lambda i: (0, 0, 0)),
            pl.BlockSpec((D, 256), lambda i: (0, i)),
            pl.BlockSpec((D, 256), lambda i: (0, i + wide)),
        ],
        out_specs=(pl.BlockSpec((ROWS, D), lambda i: (0, 0)), part, part, part),
        compiler_params=params(),
        cost_estimate=cost(4 * ROWS * D * FF, 4 * ROWS * D + 4 * D * FF + 10 * ROWS * FF),
    )(packed, weight_in, weight_in)


def down_kernel(hidden_ref, weight_ref, out_ref, last_ref):
    step = pl.program_id(0)
    values = dot(hidden_ref[...], weight_ref[...]).astype(BF16)
    pack_columns(values, step * 2, out_ref, last_ref)

    @pl.when(step == pl.num_programs(0) - 1)
    def _():
        pack_last(out_ref, last_ref)


def down(hidden, weight_out):
    return pl.pallas_call(
        down_kernel,
        grid=(D // 256,),
        out_shape=jax.ShapeDtypeStruct((BLOCKS, PACK, LANES), BF16),
        in_specs=[
            pl.BlockSpec((ROWS, FF), lambda i: (0, 0)),
            pl.BlockSpec((FF, 256), lambda i: (0, i)),
        ],
        out_specs=pl.BlockSpec((BLOCKS, PACK, LANES), lambda i: (0, 0, 0)),
        scratch_shapes=[pltpu.VMEM((BLOCKS * COLS, LANES), BF16)],
        compiler_params=params(),
        cost_estimate=cost(2 * ROWS * D * FF, 2 * ROWS * D + 2 * D * FF + 2 * ROWS * FF),
    )(hidden, weight_out)


def mix_kernel(packed_ref, weight_ref, gate_ref, up_ref, after_ref, rows_ref, gate_grad_ref, up_grad_ref):
    @pl.when(pl.program_id(0) == 0)
    def _():
        unpack_rows(packed_ref, rows_ref)

    grad = dot_nt(rows_ref[...], weight_ref[...])
    gate = gate_ref[...]
    sigma = jax.nn.sigmoid(gate)
    slope = sigma * (1.0 + gate * (1.0 - sigma))
    gate_grad_ref[...] = (grad * up_ref[...] * slope).astype(BF16)
    up_grad_ref[...] = (grad * gate * sigma).astype(BF16)


def mix(packed, weight_out, gate, up, after):
    part = pl.BlockSpec((ROWS, 256), lambda i: (0, i))
    return pl.pallas_call(
        mix_kernel,
        grid=(FF // 256,),
        out_shape=(
            jax.ShapeDtypeStruct((ROWS, D), BF16),
            jax.ShapeDtypeStruct((ROWS, FF), BF16),
            jax.ShapeDtypeStruct((ROWS, FF), BF16),
        ),
        in_specs=[
            pl.BlockSpec((BLOCKS, PACK, LANES), lambda i: (0, 0, 0)),
            pl.BlockSpec((256, D), lambda i: (i, 0)),
            part,
            part,
            STAYS,
        ],
        out_specs=(pl.BlockSpec((ROWS, D), lambda i: (0, 0)), part, part),
        compiler_params=params(),
        cost_estimate=cost(2 * ROWS * D * FF, 4 * ROWS * D + 2 * D * FF + 12 * ROWS * FF),
    )(packed, weight_out, gate, up, after)


def input_grad_kernel(gate_grad_ref, up_grad_ref, weight_ref, after_in, after_out, out_ref, last_ref):
    step = pl.program_id(0)
    values = dot_nt(gate_grad_ref[...], weight_ref[:, :FF])
    values = (values + dot_nt(up_grad_ref[...], weight_ref[:, FF:])).astype(BF16)
    pack_columns(values, step * 2, out_ref, last_ref)

    @pl.when(step == pl.num_programs(0) - 1)
    def _():
        pack_last(out_ref, last_ref)


def input_grads(gate_grad, up_grad, weight_in, after):
    whole = pl.BlockSpec((ROWS, FF), lambda i: (0, 0))
    return pl.pallas_call(
        input_grad_kernel,
        grid=(D // 256,),
        out_shape=jax.ShapeDtypeStruct((BLOCKS, PACK, LANES), BF16),
        in_specs=[whole, whole, pl.BlockSpec((256, 2 * FF), lambda i: (i, 0)), STAYS, STAYS],
        out_specs=pl.BlockSpec((BLOCKS, PACK, LANES), lambda i: (0, 0, 0)),
        scratch_shapes=[pltpu.VMEM((BLOCKS * COLS, LANES), BF16)],
        compiler_params=params(),
        cost_estimate=cost(4 * ROWS * D * FF, 2 * ROWS * D + 4 * D * FF + 4 * ROWS * FF),
    )(gate_grad, up_grad, weight_in, *after)


def weight_in_kernel(share_ref, noise_ref, rows_ref, gate_grad_ref, up_grad_ref, after_ref, out_ref):
    tile = share_ref[pl.program_id(0)] * 2 + pl.program_id(1)
    for half, grad_ref in enumerate((gate_grad_ref, up_grad_ref)):
        raw = dot_tn(rows_ref[...], grad_ref[...])
        for c in range(FF // 256):
            at = half * FF + c * 256
            scaled = raw[:, c * 256 : (c + 1) * 256] * noise_ref[tile, half * (FF // 256) + c]
            out_ref[0, :, at : at + 256] = scaled.astype(out_ref.dtype)


def weight_in_grads(shares, noise, rows, gate_grad, up_grad, dtype, after):
    whole = pl.BlockSpec((ROWS, FF), lambda j, i, s: (0, 0))
    return pl.pallas_call(
        weight_in_kernel,
        grid_spec=pltpu.PrefetchScalarGridSpec(
            num_scalar_prefetch=1,
            grid=(2, 2),
            in_specs=[
                pl.BlockSpec(memory_space=pltpu.SMEM),
                pl.BlockSpec((ROWS, 256), lambda j, i, s: (0, s[j] * 2 + i)),
                whole,
                whole,
                STAYS,
            ],
            out_specs=pl.BlockSpec((1, 256, 2 * FF), lambda j, i, s: (j, i, 0)),
        ),
        out_shape=jax.ShapeDtypeStruct((2, 512, 2 * FF), dtype),
        compiler_params=params(),
        cost_estimate=cost(2 * ROWS * D * FF, ROWS * D + 4 * ROWS * FF + 4 * D * FF),
    )(shares, noise, rows, gate_grad, up_grad, after)


def weight_out_kernel(share_ref, noise_ref, hidden_ref, rows_ref, out_ref):
    tile = share_ref[pl.program_id(0)] * 2 + pl.program_id(1)
    raw = dot_tn(hidden_ref[...], rows_ref[...])
    for c in range(FF // 256):
        cut = slice(c * 256, (c + 1) * 256)
        out_ref[0, cut, :] = (raw[cut] * noise_ref[c, tile]).astype(out_ref.dtype)


def weight_out_grads(shares, noise, hidden, rows, dtype):
    return pl.pallas_call(
        weight_out_kernel,
        grid_spec=pltpu.PrefetchScalarGridSpec(
            num_scalar_prefetch=1,
            grid=(2, 2),
            in_specs=[
                pl.BlockSpec(memory_space=pltpu.SMEM),
                pl.BlockSpec((ROWS, FF), lambda j, i, s: (0, 0)),
                pl.BlockSpec((ROWS, 256), lambda j, i, s: (0, s[j] * 2 + i)),
            ],
            out_specs=pl.BlockSpec((1, FF, 256), lambda j, i, s: (j, 0, i)),
        ),
        out_shape=jax.ShapeDtypeStruct((2, FF, 512), dtype),
        compiler_params=params(),
        cost_estimate=cost(ROWS * D * FF, ROWS * D + 2 * ROWS * FF + 2 * D * FF),
    )(shares, noise, hidden, rows)


def combine_tables(key, weight):
    key = key.T
    spread = jnp.where(iota((LANES, BIG), 1) // MAIN == iota((LANES, BIG), 0), 1.0, 0.0).astype(BF16)
    hit = dot(key.astype(BF16), spread) == (iota((TOK, BIG), 1) % MAIN).astype(F32)
    last_hit = key == float(MAIN)
    if weight is None:
        pick = jnp.where(hit, 1.0, 0.0)
        last_pick = jnp.where(last_hit, 1.0, 0.0)
    else:
        weight = weight.T
        pick = jnp.where(hit, dot(weight.astype(BF16), spread), 0.0)
        last_pick = jnp.where(last_hit, weight, 0.0)
    return pick.astype(BF16), last_pick[:, :BLOCKS].astype(BF16)


def combine_kernel(plane_ref, routes_ref, packed_ref, *refs):
    out_ref = refs[-1]
    experts = BLOCKS // 2
    key = slot_keys(routes_ref[...]).T + 1.0
    plane = plane_ref[0]

    def spread(shape, width):
        return jnp.where(iota(shape, 0) == iota(shape, 1) // width * 2 + plane, 1.0, 0.0).astype(BF16)

    main = (TOK, experts * MAIN)
    hit = dot(key.astype(BF16), spread((LANES, experts * MAIN), MAIN))
    pick = jnp.where(hit == (iota(main, 1) % MAIN + 1).astype(F32), 1.0, 0.0).astype(BF16)
    hit = dot(key.astype(BF16), spread((LANES, LANES), 1))
    last_pick = jnp.where(hit == float(MAIN + 1), 1.0, 0.0).astype(BF16)[:, :experts]

    count = experts * COLS
    row, tile = iota((count, count), 0), iota((count, count), 1)
    order = ((tile // COLS) == (row % experts)) & ((tile % COLS) == (row // experts))
    last = packed_ref[:, 0, MAIN * COLS :, :].reshape(count, LANES)
    last = dot(jnp.where(order, 1.0, 0.0).astype(BF16), last).astype(BF16)
    for j in range(COLS):
        rows = packed_ref[:, 0, j * MAIN : (j + 1) * MAIN, :].reshape(experts * MAIN, LANES)
        total = dot(pick, rows) + dot(last_pick, last[j * experts : (j + 1) * experts])
        out_ref[:, j * LANES : (j + 1) * LANES] = total.astype(out_ref.dtype)


def combine(plane, own, routes, packed, dtype, after):
    experts = BLOCKS // 2
    return pl.pallas_call(
        combine_kernel,
        grid_spec=pltpu.PrefetchScalarGridSpec(
            num_scalar_prefetch=1,
            grid=(1,),
            in_specs=[
                pl.BlockSpec((TOP, TOK), lambda i, p: (0, 0)),
                pl.BlockSpec((experts, 1, PACK, LANES), lambda i, p: (0, p[0] if own else 1 - p[0], 0, 0)),
                *[STAYS] * len(after),
            ],
            out_specs=pl.BlockSpec((TOK, D), lambda i, p: (0, 0)),
        ),
        out_shape=jax.ShapeDtypeStruct((TOK, D), dtype),
        compiler_params=params(),
        cost_estimate=cost(ROWS * TOK * D, (ROWS + 2 * TOK) * D),
    )(plane, routes, packed.reshape(experts, 2, PACK, LANES), *after)


def finish_kernel(near_ref, far_ref, after_ref, out_ref):
    out_ref[...] = (near_ref[...] + far_ref[...].astype(F32)) * 0.25


def finish(near, far, rows, after):
    height, breadth = far.shape
    part = pl.BlockSpec((rows, breadth), lambda i: (i, 0))
    return pl.pallas_call(
        finish_kernel,
        grid=(height // rows,),
        out_shape=jax.ShapeDtypeStruct((height, breadth), F32),
        in_specs=[part, part, STAYS],
        out_specs=part,
        compiler_params=params(),
        cost_estimate=cost(2 * height * breadth, 10 * height * breadth),
    )(near, far, after)


def near_kernel(kept_ref, got_ref, after_ref, out_ref):
    out_ref[...] = kept_ref[0] + got_ref[0].astype(F32)


def near_sum(kept, got, rows, after):
    _, height, breadth = kept.shape
    first = pl.BlockSpec((1, rows, breadth), lambda i: (0, i, 0))
    return pl.pallas_call(
        near_kernel,
        grid=(height // rows,),
        out_shape=jax.ShapeDtypeStruct((height, breadth), F32),
        in_specs=[first, first, STAYS],
        out_specs=pl.BlockSpec((rows, breadth), lambda i: (i, 0)),
        compiler_params=params(),
        cost_estimate=cost(height * breadth, 10 * height * breadth),
    )(kept, got, after)


def combine_output_kernel(
    routes_ref, probs_ref, cotangent_ref, packed_ref, after_in, after_out,
    out_ref, grad_ref, same_routes_ref, rows_ref,
):
    routes = routes_ref[...]
    same_routes_ref[...] = routes
    unpack_rows(packed_ref, rows_ref)
    key = slot_keys(routes)
    pick, last_pick = combine_tables(key, expert_weights(routes, probs_ref[...]))
    for j in range(D // 256):
        cut = slice(j * 256, (j + 1) * 256)
        total = dot(pick, rows_ref[:BIG, cut]) + dot(last_pick, rows_ref[BIG:, cut])
        out_ref[:, cut] = total.astype(BF16)
    main = dot_nt(rows_ref[:BIG, :], cotangent_ref[...])
    last = dot_nt(rows_ref[BIG:, :], cotangent_ref[...])
    for k in range(TOP):
        expert = routes[k : k + 1, :]
        slot = jnp.sum(jnp.where(expert == iota((LANES, TOK), 0), key, 0.0), axis=0, keepdims=True)
        slot = slot.astype(jnp.int32)
        row = jnp.where(slot < MAIN, expert * MAIN + slot, -1)
        value = jnp.sum(jnp.where(iota((BIG, TOK), 0) == row, main, 0.0), axis=0, keepdims=True)
        row = jnp.where(slot < MAIN, -1, expert)
        value += jnp.sum(jnp.where(iota((BLOCKS, TOK), 0) == row, last, 0.0), axis=0, keepdims=True)
        grad_ref[k : k + 1, :] = value


def combine_output(routes, probs, cotangent, packed, after):
    return pl.pallas_call(
        combine_output_kernel,
        out_shape=(
            jax.ShapeDtypeStruct((TOK, D), BF16),
            jax.ShapeDtypeStruct((TOP, TOK), F32),
            jax.ShapeDtypeStruct((TOP, TOK), jnp.int32),
        ),
        in_specs=[pl.BlockSpec(memory_space=pltpu.VMEM)] * 4 + [STAYS, STAYS],
        scratch_shapes=[pltpu.VMEM((ROWS, D), BF16)],
        compiler_params=params(),
        cost_estimate=cost(4 * ROWS * TOK * D, 2 * (ROWS + 2 * TOK) * D),
    )(routes, probs, cotangent, packed, *after)


def exchange(value):
    return lax.all_to_all(value, "expert", split_axis=0, concat_axis=0, tiled=True)


def exchange_in_plane(value):
    planes = [list(range(z, BLOCKS, 2)) for z in range(2)]
    value = value.reshape(BLOCKS // 2, 2 * PACK, LANES)
    return lax.all_to_all(
        value, "expert", split_axis=0, concat_axis=0, tiled=True, axis_index_groups=planes
    )


def between_planes(value):
    return lax.ppermute(value, "expert", [(e, e ^ 1) for e in range(BLOCKS)])


def across(value, flip):
    pairs = [(s * BLOCKS + e, (s ^ flip) * BLOCKS + e) for s in range(4) for e in range(BLOCKS)]
    return lax.ppermute(value, ("sample", "expert"), pairs)


def shards(tokens, routes, probs, cotangent, w_gate_up, w_down, gu_noise, down_noise):
    routes, probs, cotangent = routes[0].T, probs[0].T, cotangent[0]
    gu_noise, down_noise = gu_noise[0, 0], down_noise[0, 0]
    sample = lax.axis_index("sample")
    ours = jnp.stack([sample, sample ^ 2]).astype(jnp.int32)
    theirs = ours ^ 1

    send_x, send_dy = dispatch(routes, probs, tokens[0], cotangent)
    recv_x = exchange(send_x)
    weight_in = noisy(w_gate_up[0], gu_noise, recv_x)
    weight_out = noisy(w_down[0], down_noise, recv_x)
    recv_dy = exchange(send_dy)
    rows_x, gate, up, hidden = gate_up(recv_x, weight_in)
    output = down(hidden, weight_out)
    back_y = exchange(output)
    rows_dy, gate_grad, up_grad = mix(recv_dy, weight_out, gate, up, output)

    sent_in = weight_in_grads(theirs, gu_noise, rows_x, gate_grad, up_grad, BF16, output)
    got_in = across(sent_in, 1)
    sent_out = weight_out_grads(theirs, down_noise, hidden, rows_dy, BF16)
    got_out = across(sent_out, 1)
    kept_in = weight_in_grads(ours, gu_noise, rows_x, gate_grad, up_grad, F32, output)
    kept_out = weight_out_grads(ours, down_noise, hidden, rows_dy, F32)
    half_in = (kept_in[1] + got_in[1].astype(F32)).astype(BF16)
    half_out = (kept_out[1] + got_out[1].astype(F32)).astype(BF16)
    far_in = across(half_in, 2)
    far_out = across(half_out, 2)
    send_dx = input_grads(gate_grad, up_grad, weight_in, (half_in, half_out))
    back_dx = exchange_in_plane(send_dx)

    near_in = near_sum(kept_in, got_in, 256, back_y)
    near_out = near_sum(kept_out, got_out, 384, back_y)
    layer_out, prob_grad, same_routes = combine_output(
        routes, probs, cotangent, back_y, (near_in, near_out)
    )
    far_routes = between_planes(same_routes)
    plane = (lax.axis_index("expert") % 2).astype(jnp.int32)[None]
    there = combine(plane, False, far_routes, back_dx, BF16, ())
    here = combine(plane, True, routes, back_dx, F32, (there,))
    grad_in = finish(near_in, far_in, 256, there)
    grad_out = finish(near_out, far_out, 384, there)
    input_grad = (here + between_planes(there).astype(F32)).astype(BF16)
    return (layer_out[None], input_grad[None], prob_grad.T[None], grad_in[None], grad_out[None])


def solution(mesh):
    tokens = P("sample", "expert", None)
    noise = P("sample", "expert", None, None)
    experts = P("expert", None, None)
    in_specs = (tokens, tokens, tokens, tokens, experts, experts, noise, noise)
    out_specs = (tokens, tokens, tokens, P("expert", "sample", None), P("expert", None, "sample"))
    return jax.shard_map(shards, mesh=mesh, in_specs=in_specs, out_specs=out_specs, check_vma=False)
```

```python
import functools

import jax
import jax.numpy as jnp
from jax import lax
from jax.experimental import pallas as pl
from jax.experimental.pallas import tpu as pltpu
from jax.sharding import PartitionSpec as P

D = 2048
FF = 768
TOP = 8
TOK = 128
BLOCKS = 32
LANES = 128
COLS = D // LANES
MAIN = 32
PACK = MAIN * COLS + COLS
ROWS = BLOCKS * (MAIN + 1)
BIG = BLOCKS * MAIN
VMEM_LIMIT = 48 * 1024 * 1024

F32 = jnp.float32
BF16 = jnp.bfloat16


def params(limit=VMEM_LIMIT):
    return pltpu.CompilerParams(vmem_limit_bytes=limit)


def cost(flops, moved):
    return pl.CostEstimate(flops=flops // 1000, bytes_accessed=moved // 1000, transcendentals=0)


def iota(shape, dim):
    return lax.broadcasted_iota(jnp.int32, shape, dim)


def dot(a, b):
    return jnp.dot(a, b, preferred_element_type=F32)


def dot_nt(a, b):
    return lax.dot_general(a, b, (((1,), (1,)), ((), ())), preferred_element_type=F32)


def dot_tn(a, b):
    return lax.dot_general(a, b, (((0,), (0,)), ((), ())), preferred_element_type=F32)


STAYS = pl.BlockSpec(memory_space=pl.ANY)


def place(expert):
    return ((((expert >> 3) + (expert >> 1)) & 3) << 3) | (expert & 7)


ORDER = sorted(range(BLOCKS), key=place)


def slot_keys(routes):
    expert = iota((LANES, TOK), 0)
    chosen = jnp.zeros((LANES, TOK), F32)
    for k in range(TOP):
        chosen = jnp.where(routes[k : k + 1, :] == expert, 1.0, chosen)
    earlier = jnp.where(iota((TOK, TOK), 0) < iota((TOK, TOK), 1), 1.0, 0.0).astype(BF16)
    rank = dot(chosen.astype(BF16), earlier)
    return jnp.where(chosen > 0.0, rank, -1.0)


def expert_weights(routes, probs):
    expert = iota((LANES, TOK), 0)
    weight = jnp.zeros((LANES, TOK), F32)
    for k in range(TOP):
        weight = jnp.where(routes[k : k + 1, :] == expert, probs[k : k + 1, :].astype(F32), weight)
    return weight


def last_slot_order(receive):
    count = BLOCKS * COLS
    tile = iota((count, count), 1 if receive else 0)
    row = iota((count, count), 0 if receive else 1)
    same = ((tile // COLS) == (row % BLOCKS)) & ((tile % COLS) == (row // BLOCKS))
    return jnp.where(same, 1.0, 0.0).astype(BF16)


def unpack_last(tile):
    flat = tile.reshape(BLOCKS * COLS, LANES)
    return dot(last_slot_order(True), flat).astype(BF16)


def dispatch_kernel(
    routes_ref, probs_ref, tokens_hbm, cotangent_hbm, x_hbm, dy_hbm,
    tokens_ref, cotangent_ref, x_ref, dy_ref, last_ref, load_sem, store_sem,
):
    loads = [
        pltpu.make_async_copy(tokens_hbm, tokens_ref, load_sem.at[0]),
        pltpu.make_async_copy(cotangent_hbm, cotangent_ref, load_sem.at[1]),
    ]
    half = MAIN * COLS // 2
    stores = []
    for made_ref, hbm in ((x_ref, x_hbm), (dy_ref, dy_hbm)):
        for cut in (pl.ds(0, half), pl.ds(half, PACK - half)):
            sem = store_sem.at[len(stores)]
            stores.append(pltpu.make_async_copy(made_ref.at[:, cut, :], hbm.at[:, cut, :], sem))
    for load in loads:
        load.start()
    routes = place(routes_ref[...])
    key = slot_keys(routes)
    weight = expert_weights(routes, probs_ref[...])
    spread = jnp.where(iota((BIG, LANES), 0) // MAIN == iota((BIG, LANES), 1), 1.0, 0.0).astype(BF16)
    hit = dot(spread, key.astype(BF16)) == (iota((BIG, TOK), 0) % MAIN).astype(F32)
    last_hit = key[:BLOCKS] == float(MAIN)
    order = last_slot_order(False)

    def fill(value_ref, pick, last_pick, out_ref, first, second):
        for j in range(0, COLS, 2):
            value = value_ref[:, j * LANES : (j + 2) * LANES]
            last = dot(last_pick, value).astype(BF16)
            for i in range(2):
                last_ref[(j + i) * BLOCKS : (j + i + 1) * BLOCKS, :] = last[:, i * LANES : (i + 1) * LANES]
        tiles = dot(order, last_ref[...]).astype(BF16)
        out_ref[:, MAIN * COLS :, :] = tiles.reshape(BLOCKS, COLS, LANES)
        for j in range(0, COLS, 2):
            rows = dot(pick, value_ref[:, j * LANES : (j + 2) * LANES]).astype(BF16)
            for i in range(2):
                cut = rows[:, i * LANES : (i + 1) * LANES].reshape(BLOCKS, MAIN, LANES)
                out_ref[:, (j + i) * MAIN : (j + i + 1) * MAIN, :] = cut
            if j + 2 == COLS // 2:
                first.start()
        second.start()

    pick = jnp.where(hit, 1.0, 0.0).astype(BF16)
    last_pick = jnp.where(last_hit, 1.0, 0.0).astype(BF16)
    loads[0].wait()
    fill(tokens_ref, pick, last_pick, x_ref, stores[0], stores[1])
    pick = jnp.where(hit, dot(spread, weight.astype(BF16)), 0.0).astype(BF16)
    last_pick = jnp.where(last_hit, weight[:BLOCKS], 0.0).astype(BF16)
    loads[1].wait()
    fill(cotangent_ref, pick, last_pick, dy_ref, stores[2], stores[3])
    for store in stores:
        store.wait()


def dispatch(routes, probs, tokens, cotangent):
    packed = jax.ShapeDtypeStruct((BLOCKS, PACK, LANES), BF16)
    choice = pl.BlockSpec((TOP, TOK), lambda i: (0, 0))
    return pl.pallas_call(
        dispatch_kernel,
        grid=(1,),
        out_shape=(packed, packed),
        in_specs=[choice, choice, STAYS, STAYS],
        out_specs=(STAYS, STAYS),
        scratch_shapes=[
            pltpu.VMEM((TOK, D), BF16),
            pltpu.VMEM((TOK, D), BF16),
            pltpu.VMEM((BLOCKS, PACK, LANES), BF16),
            pltpu.VMEM((BLOCKS, PACK, LANES), BF16),
            pltpu.VMEM((BLOCKS * COLS, LANES), BF16),
            pltpu.SemaphoreType.DMA((2,)),
            pltpu.SemaphoreType.DMA((4,)),
        ],
        compiler_params=params(60 * 1024 * 1024),
        cost_estimate=cost(4 * ROWS * TOK * D, 4 * (ROWS + TOK) * D),
    )(routes, probs, tokens, cotangent)


def noisy_kernel(noise_ref, weight_ref, after_ref, out_ref):
    row = pl.program_id(0)
    for c in range(weight_ref.shape[1] // 256):
        cut = slice(c * 256, (c + 1) * 256)
        out_ref[:, cut] = (weight_ref[:, cut].astype(F32) * noise_ref[row, c]).astype(BF16)


def noisy(weight, noise, after):
    height, breadth = weight.shape
    return pl.pallas_call(
        noisy_kernel,
        grid=(height // 256,),
        out_shape=jax.ShapeDtypeStruct(weight.shape, BF16),
        in_specs=[
            pl.BlockSpec(memory_space=pltpu.SMEM),
            pl.BlockSpec((256, breadth), lambda i: (i, 0)),
            STAYS,
        ],
        out_specs=pl.BlockSpec((256, breadth), lambda i: (i, 0)),
        compiler_params=params(),
        cost_estimate=cost(height * breadth, 4 * height * breadth),
    )(noise, weight, after)


def unpack_rows(packed_ref, rows_ref):
    last = unpack_last(packed_ref[:, MAIN * COLS :, :])
    for j in range(COLS):
        cut = slice(j * LANES, (j + 1) * LANES)
        rows_ref[:BIG, cut] = packed_ref[:, j * MAIN : (j + 1) * MAIN, :].reshape(BIG, LANES)
        rows_ref[BIG:, cut] = last[j * BLOCKS : (j + 1) * BLOCKS]


def pack_columns(values, first, out_ref, last_ref):
    for i in range(2):
        cut = values[:, i * LANES : (i + 1) * LANES]
        at = pl.multiple_of((first + i) * MAIN, MAIN)
        out_ref[:, pl.ds(at, MAIN), :] = cut[:BIG].reshape(BLOCKS, MAIN, LANES)
        last_ref[pl.ds(at, BLOCKS), :] = cut[BIG:]


def pack_last(out_ref, last_ref):
    tiles = dot(last_slot_order(False), last_ref[...]).astype(BF16)
    out_ref[:, MAIN * COLS :, :] = tiles.reshape(BLOCKS, COLS, LANES)


def gate_up_kernel(packed_ref, gate_w_ref, up_w_ref, rows_ref, gate_ref, up_ref, hidden_ref):
    @pl.when(pl.program_id(0) == 0)
    def _():
        unpack_rows(packed_ref, rows_ref)

    gate = dot(rows_ref[...], gate_w_ref[...])
    gate_ref[...] = gate
    up = dot(rows_ref[...], up_w_ref[...])
    up_ref[...] = up
    hidden_ref[...] = (gate * jax.nn.sigmoid(gate) * up).astype(BF16)


def gate_up(packed, weight_in):
    wide = FF // 256
    part = pl.BlockSpec((ROWS, 256), lambda i: (0, i))
    return pl.pallas_call(
        gate_up_kernel,
        grid=(wide,),
        out_shape=(
            jax.ShapeDtypeStruct((ROWS, D), BF16),
            jax.ShapeDtypeStruct((ROWS, FF), F32),
            jax.ShapeDtypeStruct((ROWS, FF), F32),
            jax.ShapeDtypeStruct((ROWS, FF), BF16),
        ),
        in_specs=[
            pl.BlockSpec((BLOCKS, PACK, LANES), lambda i: (0, 0, 0)),
            pl.BlockSpec((D, 256), lambda i: (0, i)),
            pl.BlockSpec((D, 256), lambda i: (0, i + wide)),
        ],
        out_specs=(pl.BlockSpec((ROWS, D), lambda i: (0, 0)), part, part, part),
        compiler_params=params(),
        cost_estimate=cost(4 * ROWS * D * FF, 4 * ROWS * D + 4 * D * FF + 10 * ROWS * FF),
    )(packed, weight_in, weight_in)


def down_kernel(hidden_ref, weight_ref, out_ref, last_ref):
    step = pl.program_id(0)
    values = dot(hidden_ref[...], weight_ref[...]).astype(BF16)
    pack_columns(values, step * 2, out_ref, last_ref)

    @pl.when(step == pl.num_programs(0) - 1)
    def _():
        pack_last(out_ref, last_ref)


def down(hidden, weight_out):
    return pl.pallas_call(
        down_kernel,
        grid=(D // 256,),
        out_shape=jax.ShapeDtypeStruct((BLOCKS, PACK, LANES), BF16),
        in_specs=[
            pl.BlockSpec((ROWS, FF), lambda i: (0, 0)),
            pl.BlockSpec((FF, 256), lambda i: (0, i)),
        ],
        out_specs=pl.BlockSpec((BLOCKS, PACK, LANES), lambda i: (0, 0, 0)),
        scratch_shapes=[pltpu.VMEM((BLOCKS * COLS, LANES), BF16)],
        compiler_params=params(),
        cost_estimate=cost(2 * ROWS * D * FF, 2 * ROWS * D + 2 * D * FF + 2 * ROWS * FF),
    )(hidden, weight_out)


def mix_kernel(packed_ref, weight_ref, gate_ref, up_ref, after_ref, rows_ref, gate_grad_ref, up_grad_ref):
    @pl.when(pl.program_id(0) == 0)
    def _():
        unpack_rows(packed_ref, rows_ref)

    grad = dot_nt(rows_ref[...], weight_ref[...])
    gate = gate_ref[...]
    sigma = jax.nn.sigmoid(gate)
    slope = sigma * (1.0 + gate * (1.0 - sigma))
    gate_grad_ref[...] = (grad * up_ref[...] * slope).astype(BF16)
    up_grad_ref[...] = (grad * gate * sigma).astype(BF16)


def mix(packed, weight_out, gate, up, after):
    part = pl.BlockSpec((ROWS, 256), lambda i: (0, i))
    return pl.pallas_call(
        mix_kernel,
        grid=(FF // 256,),
        out_shape=(
            jax.ShapeDtypeStruct((ROWS, D), BF16),
            jax.ShapeDtypeStruct((ROWS, FF), BF16),
            jax.ShapeDtypeStruct((ROWS, FF), BF16),
        ),
        in_specs=[
            pl.BlockSpec((BLOCKS, PACK, LANES), lambda i: (0, 0, 0)),
            pl.BlockSpec((256, D), lambda i: (i, 0)),
            part,
            part,
            STAYS,
        ],
        out_specs=(pl.BlockSpec((ROWS, D), lambda i: (0, 0)), part, part),
        compiler_params=params(),
        cost_estimate=cost(2 * ROWS * D * FF, 4 * ROWS * D + 2 * D * FF + 12 * ROWS * FF),
    )(packed, weight_out, gate, up, after)


def input_grad_kernel(gate_grad_ref, up_grad_ref, weight_ref, after_in, after_out, out_ref, last_ref):
    step = pl.program_id(0)
    values = dot_nt(gate_grad_ref[...], weight_ref[:, :FF])
    values = (values + dot_nt(up_grad_ref[...], weight_ref[:, FF:])).astype(BF16)
    pack_columns(values, step * 2, out_ref, last_ref)

    @pl.when(step == pl.num_programs(0) - 1)
    def _():
        pack_last(out_ref, last_ref)


def input_grads(gate_grad, up_grad, weight_in, after):
    whole = pl.BlockSpec((ROWS, FF), lambda i: (0, 0))
    return pl.pallas_call(
        input_grad_kernel,
        grid=(D // 256,),
        out_shape=jax.ShapeDtypeStruct((BLOCKS, PACK, LANES), BF16),
        in_specs=[whole, whole, pl.BlockSpec((256, 2 * FF), lambda i: (i, 0)), STAYS, STAYS],
        out_specs=pl.BlockSpec((BLOCKS, PACK, LANES), lambda i: (0, 0, 0)),
        scratch_shapes=[pltpu.VMEM((BLOCKS * COLS, LANES), BF16)],
        compiler_params=params(),
        cost_estimate=cost(4 * ROWS * D * FF, 2 * ROWS * D + 4 * D * FF + 4 * ROWS * FF),
    )(gate_grad, up_grad, weight_in, *after)


def weight_in_kernel(share_ref, noise_ref, rows_ref, gate_grad_ref, up_grad_ref, after_ref, out_ref):
    tile = share_ref[pl.program_id(0)] * 2 + pl.program_id(1)
    for half, grad_ref in enumerate((gate_grad_ref, up_grad_ref)):
        raw = dot_tn(rows_ref[...], grad_ref[...])
        for c in range(FF // 256):
            at = half * FF + c * 256
            scaled = raw[:, c * 256 : (c + 1) * 256] * noise_ref[tile, half * (FF // 256) + c]
            out_ref[0, :, at : at + 256] = scaled.astype(out_ref.dtype)


def weight_in_grads(shares, noise, rows, gate_grad, up_grad, dtype, after):
    whole = pl.BlockSpec((ROWS, FF), lambda j, i, s: (0, 0))
    return pl.pallas_call(
        weight_in_kernel,
        grid_spec=pltpu.PrefetchScalarGridSpec(
            num_scalar_prefetch=1,
            grid=(2, 2),
            in_specs=[
                pl.BlockSpec(memory_space=pltpu.SMEM),
                pl.BlockSpec((ROWS, 256), lambda j, i, s: (0, s[j] * 2 + i)),
                whole,
                whole,
                STAYS,
            ],
            out_specs=pl.BlockSpec((1, 256, 2 * FF), lambda j, i, s: (j, i, 0)),
        ),
        out_shape=jax.ShapeDtypeStruct((2, 512, 2 * FF), dtype),
        compiler_params=params(),
        cost_estimate=cost(2 * ROWS * D * FF, ROWS * D + 4 * ROWS * FF + 4 * D * FF),
    )(shares, noise, rows, gate_grad, up_grad, after)


def weight_out_kernel(share_ref, noise_ref, hidden_ref, rows_ref, out_ref):
    tile = share_ref[pl.program_id(0)] * 2 + pl.program_id(1)
    raw = dot_tn(hidden_ref[...], rows_ref[...])
    for c in range(FF // 256):
        cut = slice(c * 256, (c + 1) * 256)
        out_ref[0, cut, :] = (raw[cut] * noise_ref[c, tile]).astype(out_ref.dtype)


def weight_out_grads(shares, noise, hidden, rows, dtype):
    return pl.pallas_call(
        weight_out_kernel,
        grid_spec=pltpu.PrefetchScalarGridSpec(
            num_scalar_prefetch=1,
            grid=(2, 2),
            in_specs=[
                pl.BlockSpec(memory_space=pltpu.SMEM),
                pl.BlockSpec((ROWS, FF), lambda j, i, s: (0, 0)),
                pl.BlockSpec((ROWS, 256), lambda j, i, s: (0, s[j] * 2 + i)),
            ],
            out_specs=pl.BlockSpec((1, FF, 256), lambda j, i, s: (j, 0, i)),
        ),
        out_shape=jax.ShapeDtypeStruct((2, FF, 512), dtype),
        compiler_params=params(),
        cost_estimate=cost(ROWS * D * FF, ROWS * D + 2 * ROWS * FF + 2 * D * FF),
    )(shares, noise, hidden, rows)


def combine_tables(key, weight):
    key = key.T
    spread = jnp.where(iota((LANES, BIG), 1) // MAIN == iota((LANES, BIG), 0), 1.0, 0.0).astype(BF16)
    hit = dot(key.astype(BF16), spread) == (iota((TOK, BIG), 1) % MAIN).astype(F32)
    last_hit = key == float(MAIN)
    if weight is None:
        pick = jnp.where(hit, 1.0, 0.0)
        last_pick = jnp.where(last_hit, 1.0, 0.0)
    else:
        weight = weight.T
        pick = jnp.where(hit, dot(weight.astype(BF16), spread), 0.0)
        last_pick = jnp.where(last_hit, weight, 0.0)
    return pick.astype(BF16), last_pick[:, :BLOCKS].astype(BF16)


def combine_kernel(plane_ref, routes_ref, packed_ref, *refs):
    out_ref = refs[-1]
    experts = BLOCKS // 2
    key = slot_keys(place(routes_ref[...])).T + 1.0
    plane = plane_ref[0]

    def spread(shape, width):
        return jnp.where(iota(shape, 0) == iota(shape, 1) // width * 2 + plane, 1.0, 0.0).astype(BF16)

    main = (TOK, experts * MAIN)
    hit = dot(key.astype(BF16), spread((LANES, experts * MAIN), MAIN))
    pick = jnp.where(hit == (iota(main, 1) % MAIN + 1).astype(F32), 1.0, 0.0).astype(BF16)
    hit = dot(key.astype(BF16), spread((LANES, LANES), 1))
    last_pick = jnp.where(hit == float(MAIN + 1), 1.0, 0.0).astype(BF16)[:, :experts]

    count = experts * COLS
    row, tile = iota((count, count), 0), iota((count, count), 1)
    order = ((tile // COLS) == (row % experts)) & ((tile % COLS) == (row // experts))
    last = packed_ref[:, 0, MAIN * COLS :, :].reshape(count, LANES)
    last = dot(jnp.where(order, 1.0, 0.0).astype(BF16), last).astype(BF16)
    for j in range(0, COLS, 2):
        rows, ends = [], []
        for at in (j, j + 1):
            part = packed_ref[:, 0, at * MAIN : (at + 1) * MAIN, :]
            rows.append(part.reshape(experts * MAIN, LANES))
            ends.append(last[at * experts : (at + 1) * experts])
        total = dot(pick, jnp.concatenate(rows, axis=1))
        total += dot(last_pick, jnp.concatenate(ends, axis=1))
        out_ref[:, j * LANES : (j + 2) * LANES] = total.astype(out_ref.dtype)


def combine(plane, own, routes, packed, dtype, after):
    experts = BLOCKS // 2
    return pl.pallas_call(
        combine_kernel,
        grid_spec=pltpu.PrefetchScalarGridSpec(
            num_scalar_prefetch=1,
            grid=(1,),
            in_specs=[
                pl.BlockSpec((TOP, TOK), lambda i, p: (0, 0)),
                pl.BlockSpec((experts, 1, PACK, LANES), lambda i, p: (0, p[0] if own else 1 - p[0], 0, 0)),
                *[STAYS] * len(after),
            ],
            out_specs=pl.BlockSpec((TOK, D), lambda i, p: (0, 0)),
        ),
        out_shape=jax.ShapeDtypeStruct((TOK, D), dtype),
        compiler_params=params(),
        cost_estimate=cost(ROWS * TOK * D, (ROWS + 2 * TOK) * D),
    )(plane, routes, packed.reshape(experts, 2, PACK, LANES), *after)


def finish_kernel(near_ref, far_ref, after_ref, out_ref):
    out_ref[...] = (near_ref[...] + far_ref[...].astype(F32)) * 0.25


def finish(near, far, rows, after):
    height, breadth = far.shape
    part = pl.BlockSpec((rows, breadth), lambda i: (i, 0))
    return pl.pallas_call(
        finish_kernel,
        grid=(height // rows,),
        out_shape=jax.ShapeDtypeStruct((height, breadth), F32),
        in_specs=[part, part, STAYS],
        out_specs=part,
        compiler_params=params(),
        cost_estimate=cost(2 * height * breadth, 10 * height * breadth),
    )(near, far, after)


def near_kernel(kept_ref, got_ref, after_ref, out_ref):
    out_ref[...] = kept_ref[0] + got_ref[0].astype(F32)


def near_sum(kept, got, rows, after):
    _, height, breadth = kept.shape
    first = pl.BlockSpec((1, rows, breadth), lambda i: (0, i, 0))
    return pl.pallas_call(
        near_kernel,
        grid=(height // rows,),
        out_shape=jax.ShapeDtypeStruct((height, breadth), F32),
        in_specs=[first, first, STAYS],
        out_specs=pl.BlockSpec((rows, breadth), lambda i: (i, 0)),
        compiler_params=params(),
        cost_estimate=cost(height * breadth, 10 * height * breadth),
    )(kept, got, after)


def combine_output_kernel(
    routes_ref, probs_ref, cotangent_ref, packed_ref, after_in, after_out,
    out_ref, grad_ref, same_routes_ref, rows_ref,
):
    routes = place(routes_ref[...])
    same_routes_ref[...] = routes_ref[...]
    unpack_rows(packed_ref, rows_ref)
    key = slot_keys(routes)
    pick, last_pick = combine_tables(key, expert_weights(routes, probs_ref[...]))
    for j in range(D // 256):
        cut = slice(j * 256, (j + 1) * 256)
        total = dot(pick, rows_ref[:BIG, cut]) + dot(last_pick, rows_ref[BIG:, cut])
        out_ref[:, cut] = total.astype(BF16)
    main = dot_nt(rows_ref[:BIG, :], cotangent_ref[...])
    last = dot_nt(rows_ref[BIG:, :], cotangent_ref[...])
    for k in range(TOP):
        expert = routes[k : k + 1, :]
        slot = jnp.sum(jnp.where(expert == iota((LANES, TOK), 0), key, 0.0), axis=0, keepdims=True)
        slot = slot.astype(jnp.int32)
        row = jnp.where(slot < MAIN, expert * MAIN + slot, -1)
        value = jnp.sum(jnp.where(iota((BIG, TOK), 0) == row, main, 0.0), axis=0, keepdims=True)
        row = jnp.where(slot < MAIN, -1, expert)
        value += jnp.sum(jnp.where(iota((BLOCKS, TOK), 0) == row, last, 0.0), axis=0, keepdims=True)
        grad_ref[k : k + 1, :] = value


def combine_output(routes, probs, cotangent, packed, after):
    return pl.pallas_call(
        combine_output_kernel,
        out_shape=(
            jax.ShapeDtypeStruct((TOK, D), BF16),
            jax.ShapeDtypeStruct((TOP, TOK), F32),
            jax.ShapeDtypeStruct((TOP, TOK), jnp.int32),
        ),
        in_specs=[pl.BlockSpec(memory_space=pltpu.VMEM)] * 4 + [STAYS, STAYS],
        scratch_shapes=[pltpu.VMEM((ROWS, D), BF16)],
        compiler_params=params(),
        cost_estimate=cost(4 * ROWS * TOK * D, 2 * (ROWS + 2 * TOK) * D),
    )(routes, probs, cotangent, packed, *after)


def exchange(value):
    return lax.all_to_all(
        value, "expert", split_axis=0, concat_axis=0, tiled=True, axis_index_groups=[ORDER]
    )


def exchange_in_plane(value):
    planes = [ORDER[z::2] for z in range(2)]
    value = value.reshape(BLOCKS // 2, 2 * PACK, LANES)
    return lax.all_to_all(
        value, "expert", split_axis=0, concat_axis=0, tiled=True, axis_index_groups=planes
    )


def between_planes(value):
    return lax.ppermute(value, "expert", [(e, e ^ 1) for e in range(BLOCKS)])


def across(value, flip):
    pairs = [(s * BLOCKS + e, (s ^ flip) * BLOCKS + e) for s in range(4) for e in range(BLOCKS)]
    return lax.ppermute(value, ("sample", "expert"), pairs)


def shards(tokens, routes, probs, cotangent, w_gate_up, w_down, gu_noise, down_noise):
    routes, probs, cotangent = routes[0].T, probs[0].T, cotangent[0]
    gu_noise, down_noise = gu_noise[0, 0], down_noise[0, 0]
    sample = lax.axis_index("sample")
    ours = jnp.stack([sample, sample ^ 2]).astype(jnp.int32)
    theirs = ours ^ 1

    send_x, send_dy = dispatch(routes, probs, tokens[0], cotangent)
    recv_x = exchange(send_x)
    weight_in = noisy(w_gate_up[0], gu_noise, recv_x)
    weight_out = noisy(w_down[0], down_noise, recv_x)
    recv_dy = exchange(send_dy)
    rows_x, gate, up, hidden = gate_up(recv_x, weight_in)
    output = down(hidden, weight_out)
    back_y = exchange(output)
    rows_dy, gate_grad, up_grad = mix(recv_dy, weight_out, gate, up, output)

    sent_in = weight_in_grads(theirs, gu_noise, rows_x, gate_grad, up_grad, BF16, output)
    got_in = across(sent_in, 1)
    sent_out = weight_out_grads(theirs, down_noise, hidden, rows_dy, BF16)
    got_out = across(sent_out, 1)
    kept_in = weight_in_grads(ours, gu_noise, rows_x, gate_grad, up_grad, F32, output)
    kept_out = weight_out_grads(ours, down_noise, hidden, rows_dy, F32)
    half_in = (kept_in[1] + got_in[1].astype(F32)).astype(BF16)
    half_out = (kept_out[1] + got_out[1].astype(F32)).astype(BF16)
    far_in = across(half_in, 2)
    far_out = across(half_out, 2)
    send_dx = input_grads(gate_grad, up_grad, weight_in, (half_in, half_out))
    back_dx = exchange_in_plane(send_dx)

    near_in = near_sum(kept_in, got_in, 256, back_y)
    near_out = near_sum(kept_out, got_out, 384, back_y)
    layer_out, prob_grad, same_routes = combine_output(
        routes, probs, cotangent, back_y, (near_in, near_out)
    )
    far_routes = between_planes(same_routes)
    plane = (lax.axis_index("expert") % 2).astype(jnp.int32)[None]
    there = combine(plane, False, far_routes, back_dx, BF16, ())
    here = combine(plane, True, routes, back_dx, F32, (there,))
    grad_in = finish(near_in, far_in, 256, there)
    grad_out = finish(near_out, far_out, 384, there)
    input_grad = (here + between_planes(there).astype(F32)).astype(BF16)
    return (layer_out[None], input_grad[None], prob_grad.T[None], grad_in[None], grad_out[None])


def solution(mesh):
    tokens = P("sample", "expert", None)
    noise = P("sample", "expert", None, None)
    experts = P("expert", None, None)
    in_specs = (tokens, tokens, tokens, tokens, experts, experts, noise, noise)
    out_specs = (tokens, tokens, tokens, P("expert", "sample", None), P("expert", None, "sample"))
    return jax.shard_map(shards, mesh=mesh, in_specs=in_specs, out_specs=out_specs, check_vma=False)
```

```python
import functools

import jax
import jax.numpy as jnp
from jax import lax
from jax.experimental import pallas as pl
from jax.experimental.pallas import tpu as pltpu
from jax.sharding import PartitionSpec as P

D = 2048
FF = 768
TOP = 8
TOK = 128
BLOCKS = 32
LANES = 128
COLS = D // LANES
MAIN = 32
PACK = MAIN * COLS + COLS
ROWS = BLOCKS * (MAIN + 1)
BIG = BLOCKS * MAIN
VMEM_LIMIT = 48 * 1024 * 1024

F32 = jnp.float32
BF16 = jnp.bfloat16


def params(limit=VMEM_LIMIT):
    return pltpu.CompilerParams(vmem_limit_bytes=limit)


def cost(flops, moved):
    return pl.CostEstimate(flops=flops // 1000, bytes_accessed=moved // 1000, transcendentals=0)


def iota(shape, dim):
    return lax.broadcasted_iota(jnp.int32, shape, dim)


def dot(a, b):
    return jnp.dot(a, b, preferred_element_type=F32)


def dot_nt(a, b):
    return lax.dot_general(a, b, (((1,), (1,)), ((), ())), preferred_element_type=F32)


def dot_tn(a, b):
    return lax.dot_general(a, b, (((0,), (0,)), ((), ())), preferred_element_type=F32)


STAYS = pl.BlockSpec(memory_space=pl.ANY)


def place(expert):
    return ((((expert >> 3) + 2 * (expert >> 1)) & 3) << 3) | (expert & 7)


def plane_place(expert):
    return ((((expert >> 3) + (expert >> 1)) & 3) << 3) | (expert & 7)


ORDER = sorted(range(BLOCKS), key=place)
PLANE_ORDER = sorted(range(BLOCKS), key=plane_place)
PLANE_PAIRS = [plane_place(device) // 2 for device in ORDER[::2]]


def slot_keys(routes):
    expert = iota((LANES, TOK), 0)
    chosen = jnp.zeros((LANES, TOK), F32)
    for k in range(TOP):
        chosen = jnp.where(routes[k : k + 1, :] == expert, 1.0, chosen)
    earlier = jnp.where(iota((TOK, TOK), 0) < iota((TOK, TOK), 1), 1.0, 0.0).astype(BF16)
    rank = dot(chosen.astype(BF16), earlier)
    return jnp.where(chosen > 0.0, rank, -1.0)


def expert_weights(routes, probs):
    expert = iota((LANES, TOK), 0)
    weight = jnp.zeros((LANES, TOK), F32)
    for k in range(TOP):
        weight = jnp.where(routes[k : k + 1, :] == expert, probs[k : k + 1, :].astype(F32), weight)
    return weight


def last_slot_order(receive):
    count = BLOCKS * COLS
    tile = iota((count, count), 1 if receive else 0)
    row = iota((count, count), 0 if receive else 1)
    same = ((tile // COLS) == (row % BLOCKS)) & ((tile % COLS) == (row // BLOCKS))
    return jnp.where(same, 1.0, 0.0).astype(BF16)


def unpack_last(tile):
    flat = tile.reshape(BLOCKS * COLS, LANES)
    return dot(last_slot_order(True), flat).astype(BF16)


def dispatch_kernel(
    routes_ref, probs_ref, tokens_hbm, cotangent_hbm, x_hbm, dy_hbm,
    tokens_ref, cotangent_ref, x_ref, dy_ref, last_ref, load_sem, store_sem,
):
    loads = [
        pltpu.make_async_copy(tokens_hbm, tokens_ref, load_sem.at[0]),
        pltpu.make_async_copy(cotangent_hbm, cotangent_ref, load_sem.at[1]),
    ]
    half = MAIN * COLS // 2
    stores = []
    for made_ref, hbm in ((x_ref, x_hbm), (dy_ref, dy_hbm)):
        for cut in (pl.ds(0, half), pl.ds(half, PACK - half)):
            sem = store_sem.at[len(stores)]
            stores.append(pltpu.make_async_copy(made_ref.at[:, cut, :], hbm.at[:, cut, :], sem))
    for load in loads:
        load.start()
    routes = place(routes_ref[...])
    key = slot_keys(routes)
    weight = expert_weights(routes, probs_ref[...])
    spread = jnp.where(iota((BIG, LANES), 0) // MAIN == iota((BIG, LANES), 1), 1.0, 0.0).astype(BF16)
    hit = dot(spread, key.astype(BF16)) == (iota((BIG, TOK), 0) % MAIN).astype(F32)
    last_hit = key[:BLOCKS] == float(MAIN)
    order = last_slot_order(False)

    def fill(value_ref, pick, last_pick, out_ref, first, second):
        for j in range(0, COLS, 2):
            value = value_ref[:, j * LANES : (j + 2) * LANES]
            last = dot(last_pick, value).astype(BF16)
            for i in range(2):
                last_ref[(j + i) * BLOCKS : (j + i + 1) * BLOCKS, :] = last[:, i * LANES : (i + 1) * LANES]
        tiles = dot(order, last_ref[...]).astype(BF16)
        out_ref[:, MAIN * COLS :, :] = tiles.reshape(BLOCKS, COLS, LANES)
        for j in range(0, COLS, 2):
            rows = dot(pick, value_ref[:, j * LANES : (j + 2) * LANES]).astype(BF16)
            for i in range(2):
                cut = rows[:, i * LANES : (i + 1) * LANES].reshape(BLOCKS, MAIN, LANES)
                out_ref[:, (j + i) * MAIN : (j + i + 1) * MAIN, :] = cut
            if j + 2 == COLS // 2:
                first.start()
        second.start()

    pick = jnp.where(hit, 1.0, 0.0).astype(BF16)
    last_pick = jnp.where(last_hit, 1.0, 0.0).astype(BF16)
    loads[0].wait()
    fill(tokens_ref, pick, last_pick, x_ref, stores[0], stores[1])
    pick = jnp.where(hit, dot(spread, weight.astype(BF16)), 0.0).astype(BF16)
    last_pick = jnp.where(last_hit, weight[:BLOCKS], 0.0).astype(BF16)
    loads[1].wait()
    fill(cotangent_ref, pick, last_pick, dy_ref, stores[2], stores[3])
    for store in stores:
        store.wait()


def dispatch(routes, probs, tokens, cotangent):
    packed = jax.ShapeDtypeStruct((BLOCKS, PACK, LANES), BF16)
    choice = pl.BlockSpec((TOP, TOK), lambda i: (0, 0))
    return pl.pallas_call(
        dispatch_kernel,
        grid=(1,),
        out_shape=(packed, packed),
        in_specs=[choice, choice, STAYS, STAYS],
        out_specs=(STAYS, STAYS),
        scratch_shapes=[
            pltpu.VMEM((TOK, D), BF16),
            pltpu.VMEM((TOK, D), BF16),
            pltpu.VMEM((BLOCKS, PACK, LANES), BF16),
            pltpu.VMEM((BLOCKS, PACK, LANES), BF16),
            pltpu.VMEM((BLOCKS * COLS, LANES), BF16),
            pltpu.SemaphoreType.DMA((2,)),
            pltpu.SemaphoreType.DMA((4,)),
        ],
        compiler_params=params(60 * 1024 * 1024),
        cost_estimate=cost(4 * ROWS * TOK * D, 4 * (ROWS + TOK) * D),
    )(routes, probs, tokens, cotangent)


def noisy_kernel(noise_ref, weight_ref, after_ref, out_ref):
    row = pl.program_id(0)
    for c in range(weight_ref.shape[1] // 256):
        cut = slice(c * 256, (c + 1) * 256)
        out_ref[:, cut] = (weight_ref[:, cut].astype(F32) * noise_ref[row, c]).astype(BF16)


def noisy(weight, noise, after):
    height, breadth = weight.shape
    return pl.pallas_call(
        noisy_kernel,
        grid=(height // 256,),
        out_shape=jax.ShapeDtypeStruct(weight.shape, BF16),
        in_specs=[
            pl.BlockSpec(memory_space=pltpu.SMEM),
            pl.BlockSpec((256, breadth), lambda i: (i, 0)),
            STAYS,
        ],
        out_specs=pl.BlockSpec((256, breadth), lambda i: (i, 0)),
        compiler_params=params(),
        cost_estimate=cost(height * breadth, 4 * height * breadth),
    )(noise, weight, after)


def unpack_rows(packed_ref, rows_ref):
    last = unpack_last(packed_ref[:, MAIN * COLS :, :])
    for j in range(COLS):
        cut = slice(j * LANES, (j + 1) * LANES)
        rows_ref[:BIG, cut] = packed_ref[:, j * MAIN : (j + 1) * MAIN, :].reshape(BIG, LANES)
        rows_ref[BIG:, cut] = last[j * BLOCKS : (j + 1) * BLOCKS]


def put_blocks(blocks, at, count, out_ref, pairs):
    if pairs is None:
        out_ref[:, pl.ds(at, count), :] = blocks
    else:
        for m, to in enumerate(pairs):
            out_ref[2 * to : 2 * to + 2, pl.ds(at, count), :] = blocks[2 * m : 2 * m + 2]


def pack_columns(values, first, out_ref, last_ref, pairs=None):
    for i in range(2):
        cut = values[:, i * LANES : (i + 1) * LANES]
        at = pl.multiple_of((first + i) * MAIN, MAIN)
        put_blocks(cut[:BIG].reshape(BLOCKS, MAIN, LANES), at, MAIN, out_ref, pairs)
        last_ref[pl.ds(at, BLOCKS), :] = cut[BIG:]


def pack_last(out_ref, last_ref, pairs=None):
    tiles = dot(last_slot_order(False), last_ref[...]).astype(BF16)
    put_blocks(tiles.reshape(BLOCKS, COLS, LANES), MAIN * COLS, COLS, out_ref, pairs)


def gate_up_kernel(packed_ref, gate_w_ref, up_w_ref, rows_ref, gate_ref, up_ref, hidden_ref):
    @pl.when(pl.program_id(0) == 0)
    def _():
        unpack_rows(packed_ref, rows_ref)

    gate = dot(rows_ref[...], gate_w_ref[...])
    gate_ref[...] = gate
    up = dot(rows_ref[...], up_w_ref[...])
    up_ref[...] = up
    hidden_ref[...] = (gate * jax.nn.sigmoid(gate) * up).astype(BF16)


def gate_up(packed, weight_in):
    wide = FF // 256
    part = pl.BlockSpec((ROWS, 256), lambda i: (0, i))
    return pl.pallas_call(
        gate_up_kernel,
        grid=(wide,),
        out_shape=(
            jax.ShapeDtypeStruct((ROWS, D), BF16),
            jax.ShapeDtypeStruct((ROWS, FF), F32),
            jax.ShapeDtypeStruct((ROWS, FF), F32),
            jax.ShapeDtypeStruct((ROWS, FF), BF16),
        ),
        in_specs=[
            pl.BlockSpec((BLOCKS, PACK, LANES), lambda i: (0, 0, 0)),
            pl.BlockSpec((D, 256), lambda i: (0, i)),
            pl.BlockSpec((D, 256), lambda i: (0, i + wide)),
        ],
        out_specs=(pl.BlockSpec((ROWS, D), lambda i: (0, 0)), part, part, part),
        compiler_params=params(),
        cost_estimate=cost(4 * ROWS * D * FF, 4 * ROWS * D + 4 * D * FF + 10 * ROWS * FF),
    )(packed, weight_in, weight_in)


def down_kernel(hidden_ref, weight_ref, out_ref, last_ref):
    step = pl.program_id(0)
    values = dot(hidden_ref[...], weight_ref[...]).astype(BF16)
    pack_columns(values, step * 2, out_ref, last_ref)

    @pl.when(step == pl.num_programs(0) - 1)
    def _():
        pack_last(out_ref, last_ref)


def down(hidden, weight_out):
    return pl.pallas_call(
        down_kernel,
        grid=(D // 256,),
        out_shape=jax.ShapeDtypeStruct((BLOCKS, PACK, LANES), BF16),
        in_specs=[
            pl.BlockSpec((ROWS, FF), lambda i: (0, 0)),
            pl.BlockSpec((FF, 256), lambda i: (0, i)),
        ],
        out_specs=pl.BlockSpec((BLOCKS, PACK, LANES), lambda i: (0, 0, 0)),
        scratch_shapes=[pltpu.VMEM((BLOCKS * COLS, LANES), BF16)],
        compiler_params=params(),
        cost_estimate=cost(2 * ROWS * D * FF, 2 * ROWS * D + 2 * D * FF + 2 * ROWS * FF),
    )(hidden, weight_out)


def mix_kernel(packed_ref, weight_ref, gate_ref, up_ref, after_ref, rows_ref, gate_grad_ref, up_grad_ref):
    @pl.when(pl.program_id(0) == 0)
    def _():
        unpack_rows(packed_ref, rows_ref)

    grad = dot_nt(rows_ref[...], weight_ref[...])
    gate = gate_ref[...]
    sigma = jax.nn.sigmoid(gate)
    slope = sigma * (1.0 + gate * (1.0 - sigma))
    gate_grad_ref[...] = (grad * up_ref[...] * slope).astype(BF16)
    up_grad_ref[...] = (grad * gate * sigma).astype(BF16)


def mix(packed, weight_out, gate, up, after):
    part = pl.BlockSpec((ROWS, 256), lambda i: (0, i))
    return pl.pallas_call(
        mix_kernel,
        grid=(FF // 256,),
        out_shape=(
            jax.ShapeDtypeStruct((ROWS, D), BF16),
            jax.ShapeDtypeStruct((ROWS, FF), BF16),
            jax.ShapeDtypeStruct((ROWS, FF), BF16),
        ),
        in_specs=[
            pl.BlockSpec((BLOCKS, PACK, LANES), lambda i: (0, 0, 0)),
            pl.BlockSpec((256, D), lambda i: (i, 0)),
            part,
            part,
            STAYS,
        ],
        out_specs=(pl.BlockSpec((ROWS, D), lambda i: (0, 0)), part, part),
        compiler_params=params(),
        cost_estimate=cost(2 * ROWS * D * FF, 4 * ROWS * D + 2 * D * FF + 12 * ROWS * FF),
    )(packed, weight_out, gate, up, after)


def input_grad_kernel(gate_grad_ref, up_grad_ref, weight_ref, after_in, after_out, out_ref, last_ref):
    step = pl.program_id(0)
    values = dot_nt(gate_grad_ref[...], weight_ref[:, :FF])
    values = (values + dot_nt(up_grad_ref[...], weight_ref[:, FF:])).astype(BF16)
    pack_columns(values, step * 2, out_ref, last_ref, PLANE_PAIRS)

    @pl.when(step == pl.num_programs(0) - 1)
    def _():
        pack_last(out_ref, last_ref, PLANE_PAIRS)


def input_grads(gate_grad, up_grad, weight_in, after):
    whole = pl.BlockSpec((ROWS, FF), lambda i: (0, 0))
    return pl.pallas_call(
        input_grad_kernel,
        grid=(D // 256,),
        out_shape=jax.ShapeDtypeStruct((BLOCKS, PACK, LANES), BF16),
        in_specs=[whole, whole, pl.BlockSpec((256, 2 * FF), lambda i: (i, 0)), STAYS, STAYS],
        out_specs=pl.BlockSpec((BLOCKS, PACK, LANES), lambda i: (0, 0, 0)),
        scratch_shapes=[pltpu.VMEM((BLOCKS * COLS, LANES), BF16)],
        compiler_params=params(),
        cost_estimate=cost(4 * ROWS * D * FF, 2 * ROWS * D + 4 * D * FF + 4 * ROWS * FF),
    )(gate_grad, up_grad, weight_in, *after)


def weight_in_kernel(share_ref, noise_ref, rows_ref, gate_grad_ref, up_grad_ref, after_ref, out_ref):
    tile = share_ref[pl.program_id(0)] * 2 + pl.program_id(1)
    for half, grad_ref in enumerate((gate_grad_ref, up_grad_ref)):
        raw = dot_tn(rows_ref[...], grad_ref[...])
        for c in range(FF // 256):
            at = half * FF + c * 256
            scaled = raw[:, c * 256 : (c + 1) * 256] * noise_ref[tile, half * (FF // 256) + c]
            out_ref[0, :, at : at + 256] = scaled.astype(out_ref.dtype)


def weight_in_grads(shares, noise, rows, gate_grad, up_grad, dtype, after):
    whole = pl.BlockSpec((ROWS, FF), lambda j, i, s: (0, 0))
    return pl.pallas_call(
        weight_in_kernel,
        grid_spec=pltpu.PrefetchScalarGridSpec(
            num_scalar_prefetch=1,
            grid=(2, 2),
            in_specs=[
                pl.BlockSpec(memory_space=pltpu.SMEM),
                pl.BlockSpec((ROWS, 256), lambda j, i, s: (0, s[j] * 2 + i)),
                whole,
                whole,
                STAYS,
            ],
            out_specs=pl.BlockSpec((1, 256, 2 * FF), lambda j, i, s: (j, i, 0)),
        ),
        out_shape=jax.ShapeDtypeStruct((2, 512, 2 * FF), dtype),
        compiler_params=params(),
        cost_estimate=cost(2 * ROWS * D * FF, ROWS * D + 4 * ROWS * FF + 4 * D * FF),
    )(shares, noise, rows, gate_grad, up_grad, after)


def weight_out_kernel(share_ref, noise_ref, hidden_ref, rows_ref, out_ref):
    tile = share_ref[pl.program_id(0)] * 2 + pl.program_id(1)
    raw = dot_tn(hidden_ref[...], rows_ref[...])
    for c in range(FF // 256):
        cut = slice(c * 256, (c + 1) * 256)
        out_ref[0, cut, :] = (raw[cut] * noise_ref[c, tile]).astype(out_ref.dtype)


def weight_out_grads(shares, noise, hidden, rows, dtype):
    return pl.pallas_call(
        weight_out_kernel,
        grid_spec=pltpu.PrefetchScalarGridSpec(
            num_scalar_prefetch=1,
            grid=(2, 2),
            in_specs=[
                pl.BlockSpec(memory_space=pltpu.SMEM),
                pl.BlockSpec((ROWS, FF), lambda j, i, s: (0, 0)),
                pl.BlockSpec((ROWS, 256), lambda j, i, s: (0, s[j] * 2 + i)),
            ],
            out_specs=pl.BlockSpec((1, FF, 256), lambda j, i, s: (j, 0, i)),
        ),
        out_shape=jax.ShapeDtypeStruct((2, FF, 512), dtype),
        compiler_params=params(),
        cost_estimate=cost(ROWS * D * FF, ROWS * D + 2 * ROWS * FF + 2 * D * FF),
    )(shares, noise, hidden, rows)


def combine_tables(key, weight):
    key = key.T
    spread = jnp.where(iota((LANES, BIG), 1) // MAIN == iota((LANES, BIG), 0), 1.0, 0.0).astype(BF16)
    hit = dot(key.astype(BF16), spread) == (iota((TOK, BIG), 1) % MAIN).astype(F32)
    last_hit = key == float(MAIN)
    if weight is None:
        pick = jnp.where(hit, 1.0, 0.0)
        last_pick = jnp.where(last_hit, 1.0, 0.0)
    else:
        weight = weight.T
        pick = jnp.where(hit, dot(weight.astype(BF16), spread), 0.0)
        last_pick = jnp.where(last_hit, weight, 0.0)
    return pick.astype(BF16), last_pick[:, :BLOCKS].astype(BF16)


def combine_kernel(plane_ref, routes_ref, packed_ref, *refs):
    out_ref = refs[-1]
    experts = BLOCKS // 2
    key = slot_keys(plane_place(routes_ref[...])).T + 1.0
    plane = plane_ref[0]

    def spread(shape, width):
        return jnp.where(iota(shape, 0) == iota(shape, 1) // width * 2 + plane, 1.0, 0.0).astype(BF16)

    main = (TOK, experts * MAIN)
    hit = dot(key.astype(BF16), spread((LANES, experts * MAIN), MAIN))
    pick = jnp.where(hit == (iota(main, 1) % MAIN + 1).astype(F32), 1.0, 0.0).astype(BF16)
    hit = dot(key.astype(BF16), spread((LANES, LANES), 1))
    last_pick = jnp.where(hit == float(MAIN + 1), 1.0, 0.0).astype(BF16)[:, :experts]

    count = experts * COLS
    row, tile = iota((count, count), 0), iota((count, count), 1)
    order = ((tile // COLS) == (row % experts)) & ((tile % COLS) == (row // experts))
    last = packed_ref[:, 0, MAIN * COLS :, :].reshape(count, LANES)
    last = dot(jnp.where(order, 1.0, 0.0).astype(BF16), last).astype(BF16)
    for j in range(0, COLS, 2):
        rows, ends = [], []
        for at in (j, j + 1):
            part = packed_ref[:, 0, at * MAIN : (at + 1) * MAIN, :]
            rows.append(part.reshape(experts * MAIN, LANES))
            ends.append(last[at * experts : (at + 1) * experts])
        total = dot(pick, jnp.concatenate(rows, axis=1))
        total += dot(last_pick, jnp.concatenate(ends, axis=1))
        out_ref[:, j * LANES : (j + 2) * LANES] = total.astype(out_ref.dtype)


def combine(plane, own, routes, packed, dtype, after):
    experts = BLOCKS // 2
    return pl.pallas_call(
        combine_kernel,
        grid_spec=pltpu.PrefetchScalarGridSpec(
            num_scalar_prefetch=1,
            grid=(1,),
            in_specs=[
                pl.BlockSpec((TOP, TOK), lambda i, p: (0, 0)),
                pl.BlockSpec((experts, 1, PACK, LANES), lambda i, p: (0, p[0] if own else 1 - p[0], 0, 0)),
                *[STAYS] * len(after),
            ],
            out_specs=pl.BlockSpec((TOK, D), lambda i, p: (0, 0)),
        ),
        out_shape=jax.ShapeDtypeStruct((TOK, D), dtype),
        compiler_params=params(),
        cost_estimate=cost(ROWS * TOK * D, (ROWS + 2 * TOK) * D),
    )(plane, routes, packed.reshape(experts, 2, PACK, LANES), *after)


def finish_kernel(near_ref, far_ref, after_ref, out_ref):
    out_ref[...] = (near_ref[...] + far_ref[...].astype(F32)) * 0.25


def finish(near, far, rows, after):
    height, breadth = far.shape
    part = pl.BlockSpec((rows, breadth), lambda i: (i, 0))
    return pl.pallas_call(
        finish_kernel,
        grid=(height // rows,),
        out_shape=jax.ShapeDtypeStruct((height, breadth), F32),
        in_specs=[part, part, STAYS],
        out_specs=part,
        compiler_params=params(),
        cost_estimate=cost(2 * height * breadth, 10 * height * breadth),
    )(near, far, after)


def near_kernel(kept_ref, got_ref, after_ref, out_ref):
    out_ref[...] = kept_ref[0] + got_ref[0].astype(F32)


def near_sum(kept, got, rows, after):
    _, height, breadth = kept.shape
    first = pl.BlockSpec((1, rows, breadth), lambda i: (0, i, 0))
    return pl.pallas_call(
        near_kernel,
        grid=(height // rows,),
        out_shape=jax.ShapeDtypeStruct((height, breadth), F32),
        in_specs=[first, first, STAYS],
        out_specs=pl.BlockSpec((rows, breadth), lambda i: (i, 0)),
        compiler_params=params(),
        cost_estimate=cost(height * breadth, 10 * height * breadth),
    )(kept, got, after)


def combine_output_kernel(
    routes_ref, probs_ref, cotangent_ref, packed_ref, after_in, after_out,
    out_ref, grad_ref, same_routes_ref, rows_ref,
):
    routes = place(routes_ref[...])
    same_routes_ref[...] = routes_ref[...]
    unpack_rows(packed_ref, rows_ref)
    key = slot_keys(routes)
    pick, last_pick = combine_tables(key, expert_weights(routes, probs_ref[...]))
    for j in range(D // 256):
        cut = slice(j * 256, (j + 1) * 256)
        total = dot(pick, rows_ref[:BIG, cut]) + dot(last_pick, rows_ref[BIG:, cut])
        out_ref[:, cut] = total.astype(BF16)
    main = dot_nt(rows_ref[:BIG, :], cotangent_ref[...])
    last = dot_nt(rows_ref[BIG:, :], cotangent_ref[...])
    for k in range(TOP):
        expert = routes[k : k + 1, :]
        slot = jnp.sum(jnp.where(expert == iota((LANES, TOK), 0), key, 0.0), axis=0, keepdims=True)
        slot = slot.astype(jnp.int32)
        row = jnp.where(slot < MAIN, expert * MAIN + slot, -1)
        value = jnp.sum(jnp.where(iota((BIG, TOK), 0) == row, main, 0.0), axis=0, keepdims=True)
        row = jnp.where(slot < MAIN, -1, expert)
        value += jnp.sum(jnp.where(iota((BLOCKS, TOK), 0) == row, last, 0.0), axis=0, keepdims=True)
        grad_ref[k : k + 1, :] = value


def combine_output(routes, probs, cotangent, packed, after):
    return pl.pallas_call(
        combine_output_kernel,
        out_shape=(
            jax.ShapeDtypeStruct((TOK, D), BF16),
            jax.ShapeDtypeStruct((TOP, TOK), F32),
            jax.ShapeDtypeStruct((TOP, TOK), jnp.int32),
        ),
        in_specs=[pl.BlockSpec(memory_space=pltpu.VMEM)] * 4 + [STAYS, STAYS],
        scratch_shapes=[pltpu.VMEM((ROWS, D), BF16)],
        compiler_params=params(),
        cost_estimate=cost(4 * ROWS * TOK * D, 2 * (ROWS + 2 * TOK) * D),
    )(routes, probs, cotangent, packed, *after)


def exchange(value):
    return lax.all_to_all(
        value, "expert", split_axis=0, concat_axis=0, tiled=True, axis_index_groups=[ORDER]
    )


def exchange_in_plane(value):
    planes = [PLANE_ORDER[z::2] for z in range(2)]
    value = value.reshape(BLOCKS // 2, 2 * PACK, LANES)
    return lax.all_to_all(
        value, "expert", split_axis=0, concat_axis=0, tiled=True, axis_index_groups=planes
    )


def between_planes(value):
    return lax.ppermute(value, "expert", [(e, e ^ 1) for e in range(BLOCKS)])


def across(value, flip):
    pairs = [(s * BLOCKS + e, (s ^ flip) * BLOCKS + e) for s in range(4) for e in range(BLOCKS)]
    return lax.ppermute(value, ("sample", "expert"), pairs)


def shards(tokens, routes, probs, cotangent, w_gate_up, w_down, gu_noise, down_noise):
    routes, probs, cotangent = routes[0].T, probs[0].T, cotangent[0]
    gu_noise, down_noise = gu_noise[0, 0], down_noise[0, 0]
    sample = lax.axis_index("sample")
    ours = jnp.stack([sample, sample ^ 2]).astype(jnp.int32)
    theirs = ours ^ 1

    send_x, send_dy = dispatch(routes, probs, tokens[0], cotangent)
    recv_x = exchange(send_x)
    weight_in = noisy(w_gate_up[0], gu_noise, recv_x)
    weight_out = noisy(w_down[0], down_noise, recv_x)
    recv_dy = exchange(send_dy)
    rows_x, gate, up, hidden = gate_up(recv_x, weight_in)
    output = down(hidden, weight_out)
    back_y = exchange(output)
    rows_dy, gate_grad, up_grad = mix(recv_dy, weight_out, gate, up, output)

    sent_in = weight_in_grads(theirs, gu_noise, rows_x, gate_grad, up_grad, BF16, output)
    got_in = across(sent_in, 1)
    sent_out = weight_out_grads(theirs, down_noise, hidden, rows_dy, BF16)
    got_out = across(sent_out, 1)
    kept_in = weight_in_grads(ours, gu_noise, rows_x, gate_grad, up_grad, F32, output)
    kept_out = weight_out_grads(ours, down_noise, hidden, rows_dy, F32)
    half_in = (kept_in[1] + got_in[1].astype(F32)).astype(BF16)
    half_out = (kept_out[1] + got_out[1].astype(F32)).astype(BF16)
    far_in = across(half_in, 2)
    far_out = across(half_out, 2)
    send_dx = input_grads(gate_grad, up_grad, weight_in, (half_in, half_out))
    back_dx = exchange_in_plane(send_dx)

    near_in = near_sum(kept_in, got_in, 256, back_y)
    near_out = near_sum(kept_out, got_out, 384, back_y)
    layer_out, prob_grad, same_routes = combine_output(
        routes, probs, cotangent, back_y, (near_in, near_out)
    )
    far_routes = between_planes(same_routes)
    plane = (lax.axis_index("expert") % 2).astype(jnp.int32)[None]
    there = combine(plane, False, far_routes, back_dx, BF16, ())
    here = combine(plane, True, routes, back_dx, F32, (there,))
    grad_in = finish(near_in, far_in, 256, there)
    grad_out = finish(near_out, far_out, 384, there)
    input_grad = (here + between_planes(there).astype(F32)).astype(BF16)
    return (layer_out[None], input_grad[None], prob_grad.T[None], grad_in[None], grad_out[None])


def solution(mesh):
    tokens = P("sample", "expert", None)
    noise = P("sample", "expert", None, None)
    experts = P("expert", None, None)
    in_specs = (tokens, tokens, tokens, tokens, experts, experts, noise, noise)
    out_specs = (tokens, tokens, tokens, P("expert", "sample", None), P("expert", None, "sample"))
    return jax.shard_map(shards, mesh=mesh, in_specs=in_specs, out_specs=out_specs, check_vma=False)
```

```python
import functools

import jax
import jax.numpy as jnp
from jax import lax
from jax.experimental import pallas as pl
from jax.experimental.pallas import tpu as pltpu
from jax.sharding import PartitionSpec as P

D = 2048
FF = 768
TOP = 8
TOK = 128
BLOCKS = 32
LANES = 128
COLS = D // LANES
MAIN = 32
PACK = MAIN * COLS + COLS
ROWS = BLOCKS * (MAIN + 1)
BIG = BLOCKS * MAIN
VMEM_LIMIT = 48 * 1024 * 1024

F32 = jnp.float32
BF16 = jnp.bfloat16


def params(limit=VMEM_LIMIT):
    return pltpu.CompilerParams(vmem_limit_bytes=limit)


def cost(flops, moved):
    return pl.CostEstimate(flops=flops // 1000, bytes_accessed=moved // 1000, transcendentals=0)


def iota(shape, dim):
    return lax.broadcasted_iota(jnp.int32, shape, dim)


def dot(a, b):
    return jnp.dot(a, b, preferred_element_type=F32)


def dot_nt(a, b):
    return lax.dot_general(a, b, (((1,), (1,)), ((), ())), preferred_element_type=F32)


def dot_tn(a, b):
    return lax.dot_general(a, b, (((0,), (0,)), ((), ())), preferred_element_type=F32)


STAYS = pl.BlockSpec(memory_space=pl.ANY)


def place(expert):
    return ((((expert >> 1) + 2 * (expert >> 3)) & 3) << 3) | ((expert >> 3) << 1) | (expert & 1)


def plane_place(expert):
    return ((((expert >> 3) + (expert >> 1)) & 3) << 3) | (expert & 7)


ORDER = sorted(range(BLOCKS), key=place)
PLANE_ORDER = sorted(range(BLOCKS), key=plane_place)
PLANE_PAIRS = [plane_place(device) // 2 for device in ORDER[::2]]


def slot_keys(routes):
    expert = iota((LANES, TOK), 0)
    chosen = jnp.zeros((LANES, TOK), F32)
    for k in range(TOP):
        chosen = jnp.where(routes[k : k + 1, :] == expert, 1.0, chosen)
    earlier = jnp.where(iota((TOK, TOK), 0) < iota((TOK, TOK), 1), 1.0, 0.0).astype(BF16)
    rank = dot(chosen.astype(BF16), earlier)
    return jnp.where(chosen > 0.0, rank, -1.0)


def expert_weights(routes, probs):
    expert = iota((LANES, TOK), 0)
    weight = jnp.zeros((LANES, TOK), F32)
    for k in range(TOP):
        weight = jnp.where(routes[k : k + 1, :] == expert, probs[k : k + 1, :].astype(F32), weight)
    return weight


def last_slot_order(receive):
    count = BLOCKS * COLS
    tile = iota((count, count), 1 if receive else 0)
    row = iota((count, count), 0 if receive else 1)
    same = ((tile // COLS) == (row % BLOCKS)) & ((tile % COLS) == (row // BLOCKS))
    return jnp.where(same, 1.0, 0.0).astype(BF16)


def unpack_last(tile):
    flat = tile.reshape(BLOCKS * COLS, LANES)
    return dot(last_slot_order(True), flat).astype(BF16)


def dispatch_kernel(
    routes_ref, probs_ref, tokens_hbm, cotangent_hbm, x_hbm, dy_hbm,
    tokens_ref, cotangent_ref, x_ref, dy_ref, last_ref, load_sem, store_sem,
):
    loads = [
        pltpu.make_async_copy(tokens_hbm, tokens_ref, load_sem.at[0]),
        pltpu.make_async_copy(cotangent_hbm, cotangent_ref, load_sem.at[1]),
    ]
    half = MAIN * COLS // 2
    stores = []
    for made_ref, hbm in ((x_ref, x_hbm), (dy_ref, dy_hbm)):
        for cut in (pl.ds(0, half), pl.ds(half, PACK - half)):
            sem = store_sem.at[len(stores)]
            stores.append(pltpu.make_async_copy(made_ref.at[:, cut, :], hbm.at[:, cut, :], sem))
    for load in loads:
        load.start()
    routes = place(routes_ref[...])
    key = slot_keys(routes)
    weight = expert_weights(routes, probs_ref[...])
    spread = jnp.where(iota((BIG, LANES), 0) // MAIN == iota((BIG, LANES), 1), 1.0, 0.0).astype(BF16)
    hit = dot(spread, key.astype(BF16)) == (iota((BIG, TOK), 0) % MAIN).astype(F32)
    last_hit = key[:BLOCKS] == float(MAIN)
    order = last_slot_order(False)

    def fill(value_ref, pick, last_pick, out_ref, first, second):
        for j in range(0, COLS, 2):
            value = value_ref[:, j * LANES : (j + 2) * LANES]
            last = dot(last_pick, value).astype(BF16)
            for i in range(2):
                last_ref[(j + i) * BLOCKS : (j + i + 1) * BLOCKS, :] = last[:, i * LANES : (i + 1) * LANES]
        tiles = dot(order, last_ref[...]).astype(BF16)
        out_ref[:, MAIN * COLS :, :] = tiles.reshape(BLOCKS, COLS, LANES)
        for j in range(0, COLS, 2):
            rows = dot(pick, value_ref[:, j * LANES : (j + 2) * LANES]).astype(BF16)
            for i in range(2):
                cut = rows[:, i * LANES : (i + 1) * LANES].reshape(BLOCKS, MAIN, LANES)
                out_ref[:, (j + i) * MAIN : (j + i + 1) * MAIN, :] = cut
            if j + 2 == COLS // 2:
                first.start()
        second.start()

    pick = jnp.where(hit, 1.0, 0.0).astype(BF16)
    last_pick = jnp.where(last_hit, 1.0, 0.0).astype(BF16)
    loads[0].wait()
    fill(tokens_ref, pick, last_pick, x_ref, stores[0], stores[1])
    pick = jnp.where(hit, dot(spread, weight.astype(BF16)), 0.0).astype(BF16)
    last_pick = jnp.where(last_hit, weight[:BLOCKS], 0.0).astype(BF16)
    loads[1].wait()
    fill(cotangent_ref, pick, last_pick, dy_ref, stores[2], stores[3])
    for store in stores:
        store.wait()


def dispatch(routes, probs, tokens, cotangent):
    packed = jax.ShapeDtypeStruct((BLOCKS, PACK, LANES), BF16)
    choice = pl.BlockSpec((TOP, TOK), lambda i: (0, 0))
    return pl.pallas_call(
        dispatch_kernel,
        grid=(1,),
        out_shape=(packed, packed),
        in_specs=[choice, choice, STAYS, STAYS],
        out_specs=(STAYS, STAYS),
        scratch_shapes=[
            pltpu.VMEM((TOK, D), BF16),
            pltpu.VMEM((TOK, D), BF16),
            pltpu.VMEM((BLOCKS, PACK, LANES), BF16),
            pltpu.VMEM((BLOCKS, PACK, LANES), BF16),
            pltpu.VMEM((BLOCKS * COLS, LANES), BF16),
            pltpu.SemaphoreType.DMA((2,)),
            pltpu.SemaphoreType.DMA((4,)),
        ],
        compiler_params=params(60 * 1024 * 1024),
        cost_estimate=cost(4 * ROWS * TOK * D, 4 * (ROWS + TOK) * D),
    )(routes, probs, tokens, cotangent)


def noisy_kernel(noise_ref, weight_ref, after_ref, out_ref):
    row = pl.program_id(0)
    for c in range(weight_ref.shape[1] // 256):
        cut = slice(c * 256, (c + 1) * 256)
        out_ref[:, cut] = (weight_ref[:, cut].astype(F32) * noise_ref[row, c]).astype(BF16)


def noisy(weight, noise, after):
    height, breadth = weight.shape
    return pl.pallas_call(
        noisy_kernel,
        grid=(height // 256,),
        out_shape=jax.ShapeDtypeStruct(weight.shape, BF16),
        in_specs=[
            pl.BlockSpec(memory_space=pltpu.SMEM),
            pl.BlockSpec((256, breadth), lambda i: (i, 0)),
            STAYS,
        ],
        out_specs=pl.BlockSpec((256, breadth), lambda i: (i, 0)),
        compiler_params=params(),
        cost_estimate=cost(height * breadth, 4 * height * breadth),
    )(noise, weight, after)


def unpack_rows(packed_ref, rows_ref):
    last = unpack_last(packed_ref[:, MAIN * COLS :, :])
    for j in range(COLS):
        cut = slice(j * LANES, (j + 1) * LANES)
        rows_ref[:BIG, cut] = packed_ref[:, j * MAIN : (j + 1) * MAIN, :].reshape(BIG, LANES)
        rows_ref[BIG:, cut] = last[j * BLOCKS : (j + 1) * BLOCKS]


def put_blocks(blocks, at, count, out_ref, pairs):
    if pairs is None:
        out_ref[:, pl.ds(at, count), :] = blocks
    else:
        for m, to in enumerate(pairs):
            out_ref[2 * to : 2 * to + 2, pl.ds(at, count), :] = blocks[2 * m : 2 * m + 2]


def pack_columns(values, first, out_ref, last_ref, pairs=None):
    for i in range(2):
        cut = values[:, i * LANES : (i + 1) * LANES]
        at = pl.multiple_of((first + i) * MAIN, MAIN)
        put_blocks(cut[:BIG].reshape(BLOCKS, MAIN, LANES), at, MAIN, out_ref, pairs)
        last_ref[pl.ds(at, BLOCKS), :] = cut[BIG:]


def pack_last(out_ref, last_ref, pairs=None):
    tiles = dot(last_slot_order(False), last_ref[...]).astype(BF16)
    put_blocks(tiles.reshape(BLOCKS, COLS, LANES), MAIN * COLS, COLS, out_ref, pairs)


def gate_up_kernel(packed_ref, gate_w_ref, up_w_ref, rows_ref, gate_ref, up_ref, hidden_ref):
    @pl.when(pl.program_id(0) == 0)
    def _():
        unpack_rows(packed_ref, rows_ref)

    gate = dot(rows_ref[...], gate_w_ref[...])
    gate_ref[...] = gate
    up = dot(rows_ref[...], up_w_ref[...])
    up_ref[...] = up
    hidden_ref[...] = (gate * jax.nn.sigmoid(gate) * up).astype(BF16)


def gate_up(packed, weight_in):
    wide = FF // 256
    part = pl.BlockSpec((ROWS, 256), lambda i: (0, i))
    return pl.pallas_call(
        gate_up_kernel,
        grid=(wide,),
        out_shape=(
            jax.ShapeDtypeStruct((ROWS, D), BF16),
            jax.ShapeDtypeStruct((ROWS, FF), F32),
            jax.ShapeDtypeStruct((ROWS, FF), F32),
            jax.ShapeDtypeStruct((ROWS, FF), BF16),
        ),
        in_specs=[
            pl.BlockSpec((BLOCKS, PACK, LANES), lambda i: (0, 0, 0)),
            pl.BlockSpec((D, 256), lambda i: (0, i)),
            pl.BlockSpec((D, 256), lambda i: (0, i + wide)),
        ],
        out_specs=(pl.BlockSpec((ROWS, D), lambda i: (0, 0)), part, part, part),
        compiler_params=params(),
        cost_estimate=cost(4 * ROWS * D * FF, 4 * ROWS * D + 4 * D * FF + 10 * ROWS * FF),
    )(packed, weight_in, weight_in)


def down_kernel(hidden_ref, weight_ref, out_ref, last_ref):
    step = pl.program_id(0)
    values = dot(hidden_ref[...], weight_ref[...]).astype(BF16)
    pack_columns(values, step * 2, out_ref, last_ref)

    @pl.when(step == pl.num_programs(0) - 1)
    def _():
        pack_last(out_ref, last_ref)


def down(hidden, weight_out):
    return pl.pallas_call(
        down_kernel,
        grid=(D // 256,),
        out_shape=jax.ShapeDtypeStruct((BLOCKS, PACK, LANES), BF16),
        in_specs=[
            pl.BlockSpec((ROWS, FF), lambda i: (0, 0)),
            pl.BlockSpec((FF, 256), lambda i: (0, i)),
        ],
        out_specs=pl.BlockSpec((BLOCKS, PACK, LANES), lambda i: (0, 0, 0)),
        scratch_shapes=[pltpu.VMEM((BLOCKS * COLS, LANES), BF16)],
        compiler_params=params(),
        cost_estimate=cost(2 * ROWS * D * FF, 2 * ROWS * D + 2 * D * FF + 2 * ROWS * FF),
    )(hidden, weight_out)


def mix_kernel(packed_ref, weight_ref, gate_ref, up_ref, after_ref, rows_ref, gate_grad_ref, up_grad_ref):
    @pl.when(pl.program_id(0) == 0)
    def _():
        unpack_rows(packed_ref, rows_ref)

    grad = dot_nt(rows_ref[...], weight_ref[...])
    gate = gate_ref[...]
    sigma = jax.nn.sigmoid(gate)
    slope = sigma * (1.0 + gate * (1.0 - sigma))
    gate_grad_ref[...] = (grad * up_ref[...] * slope).astype(BF16)
    up_grad_ref[...] = (grad * gate * sigma).astype(BF16)


def mix(packed, weight_out, gate, up, after):
    part = pl.BlockSpec((ROWS, 256), lambda i: (0, i))
    return pl.pallas_call(
        mix_kernel,
        grid=(FF // 256,),
        out_shape=(
            jax.ShapeDtypeStruct((ROWS, D), BF16),
            jax.ShapeDtypeStruct((ROWS, FF), BF16),
            jax.ShapeDtypeStruct((ROWS, FF), BF16),
        ),
        in_specs=[
            pl.BlockSpec((BLOCKS, PACK, LANES), lambda i: (0, 0, 0)),
            pl.BlockSpec((256, D), lambda i: (i, 0)),
            part,
            part,
            STAYS,
        ],
        out_specs=(pl.BlockSpec((ROWS, D), lambda i: (0, 0)), part, part),
        compiler_params=params(),
        cost_estimate=cost(2 * ROWS * D * FF, 4 * ROWS * D + 2 * D * FF + 12 * ROWS * FF),
    )(packed, weight_out, gate, up, after)


def input_grad_kernel(gate_grad_ref, up_grad_ref, weight_ref, after_in, after_out, out_ref, last_ref):
    step = pl.program_id(0)
    values = dot_nt(gate_grad_ref[...], weight_ref[:, :FF])
    values = (values + dot_nt(up_grad_ref[...], weight_ref[:, FF:])).astype(BF16)
    pack_columns(values, step * 2, out_ref, last_ref, PLANE_PAIRS)

    @pl.when(step == pl.num_programs(0) - 1)
    def _():
        pack_last(out_ref, last_ref, PLANE_PAIRS)


def input_grads(gate_grad, up_grad, weight_in, after):
    whole = pl.BlockSpec((ROWS, FF), lambda i: (0, 0))
    return pl.pallas_call(
        input_grad_kernel,
        grid=(D // 256,),
        out_shape=jax.ShapeDtypeStruct((BLOCKS, PACK, LANES), BF16),
        in_specs=[whole, whole, pl.BlockSpec((256, 2 * FF), lambda i: (i, 0)), STAYS, STAYS],
        out_specs=pl.BlockSpec((BLOCKS, PACK, LANES), lambda i: (0, 0, 0)),
        scratch_shapes=[pltpu.VMEM((BLOCKS * COLS, LANES), BF16)],
        compiler_params=params(),
        cost_estimate=cost(4 * ROWS * D * FF, 2 * ROWS * D + 4 * D * FF + 4 * ROWS * FF),
    )(gate_grad, up_grad, weight_in, *after)


def weight_in_kernel(share_ref, noise_ref, rows_ref, gate_grad_ref, up_grad_ref, after_ref, out_ref):
    tile = share_ref[pl.program_id(0)] * 2 + pl.program_id(1)
    for half, grad_ref in enumerate((gate_grad_ref, up_grad_ref)):
        raw = dot_tn(rows_ref[...], grad_ref[...])
        for c in range(FF // 256):
            at = half * FF + c * 256
            scaled = raw[:, c * 256 : (c + 1) * 256] * noise_ref[tile, half * (FF // 256) + c]
            out_ref[0, :, at : at + 256] = scaled.astype(out_ref.dtype)


def weight_in_grads(shares, noise, rows, gate_grad, up_grad, dtype, after):
    whole = pl.BlockSpec((ROWS, FF), lambda j, i, s: (0, 0))
    return pl.pallas_call(
        weight_in_kernel,
        grid_spec=pltpu.PrefetchScalarGridSpec(
            num_scalar_prefetch=1,
            grid=(2, 2),
            in_specs=[
                pl.BlockSpec(memory_space=pltpu.SMEM),
                pl.BlockSpec((ROWS, 256), lambda j, i, s: (0, s[j] * 2 + i)),
                whole,
                whole,
                STAYS,
            ],
            out_specs=pl.BlockSpec((1, 256, 2 * FF), lambda j, i, s: (j, i, 0)),
        ),
        out_shape=jax.ShapeDtypeStruct((2, 512, 2 * FF), dtype),
        compiler_params=params(),
        cost_estimate=cost(2 * ROWS * D * FF, ROWS * D + 4 * ROWS * FF + 4 * D * FF),
    )(shares, noise, rows, gate_grad, up_grad, after)


def weight_out_kernel(share_ref, noise_ref, hidden_ref, rows_ref, out_ref):
    tile = share_ref[pl.program_id(0)] * 2 + pl.program_id(1)
    raw = dot_tn(hidden_ref[...], rows_ref[...])
    for c in range(FF // 256):
        cut = slice(c * 256, (c + 1) * 256)
        out_ref[0, cut, :] = (raw[cut] * noise_ref[c, tile]).astype(out_ref.dtype)


def weight_out_grads(shares, noise, hidden, rows, dtype):
    return pl.pallas_call(
        weight_out_kernel,
        grid_spec=pltpu.PrefetchScalarGridSpec(
            num_scalar_prefetch=1,
            grid=(2, 2),
            in_specs=[
                pl.BlockSpec(memory_space=pltpu.SMEM),
                pl.BlockSpec((ROWS, FF), lambda j, i, s: (0, 0)),
                pl.BlockSpec((ROWS, 256), lambda j, i, s: (0, s[j] * 2 + i)),
            ],
            out_specs=pl.BlockSpec((1, FF, 256), lambda j, i, s: (j, 0, i)),
        ),
        out_shape=jax.ShapeDtypeStruct((2, FF, 512), dtype),
        compiler_params=params(),
        cost_estimate=cost(ROWS * D * FF, ROWS * D + 2 * ROWS * FF + 2 * D * FF),
    )(shares, noise, hidden, rows)


def combine_tables(key, weight):
    key = key.T
    spread = jnp.where(iota((LANES, BIG), 1) // MAIN == iota((LANES, BIG), 0), 1.0, 0.0).astype(BF16)
    hit = dot(key.astype(BF16), spread) == (iota((TOK, BIG), 1) % MAIN).astype(F32)
    last_hit = key == float(MAIN)
    if weight is None:
        pick = jnp.where(hit, 1.0, 0.0)
        last_pick = jnp.where(last_hit, 1.0, 0.0)
    else:
        weight = weight.T
        pick = jnp.where(hit, dot(weight.astype(BF16), spread), 0.0)
        last_pick = jnp.where(last_hit, weight, 0.0)
    return pick.astype(BF16), last_pick[:, :BLOCKS].astype(BF16)


def combine_kernel(plane_ref, routes_ref, packed_ref, *refs):
    out_ref = refs[-1]
    experts = BLOCKS // 2
    key = slot_keys(plane_place(routes_ref[...])).T + 1.0
    plane = plane_ref[0]

    def spread(shape, width):
        return jnp.where(iota(shape, 0) == iota(shape, 1) // width * 2 + plane, 1.0, 0.0).astype(BF16)

    main = (TOK, experts * MAIN)
    hit = dot(key.astype(BF16), spread((LANES, experts * MAIN), MAIN))
    pick = jnp.where(hit == (iota(main, 1) % MAIN + 1).astype(F32), 1.0, 0.0).astype(BF16)
    hit = dot(key.astype(BF16), spread((LANES, LANES), 1))
    last_pick = jnp.where(hit == float(MAIN + 1), 1.0, 0.0).astype(BF16)[:, :experts]

    count = experts * COLS
    row, tile = iota((count, count), 0), iota((count, count), 1)
    order = ((tile // COLS) == (row % experts)) & ((tile % COLS) == (row // experts))
    last = packed_ref[:, 0, MAIN * COLS :, :].reshape(count, LANES)
    last = dot(jnp.where(order, 1.0, 0.0).astype(BF16), last).astype(BF16)
    for j in range(0, COLS, 2):
        rows, ends = [], []
        for at in (j, j + 1):
            part = packed_ref[:, 0, at * MAIN : (at + 1) * MAIN, :]
            rows.append(part.reshape(experts * MAIN, LANES))
            ends.append(last[at * experts : (at + 1) * experts])
        total = dot(pick, jnp.concatenate(rows, axis=1))
        total += dot(last_pick, jnp.concatenate(ends, axis=1))
        out_ref[:, j * LANES : (j + 2) * LANES] = total.astype(out_ref.dtype)


def combine(plane, own, routes, packed, dtype, after):
    experts = BLOCKS // 2
    return pl.pallas_call(
        combine_kernel,
        grid_spec=pltpu.PrefetchScalarGridSpec(
            num_scalar_prefetch=1,
            grid=(1,),
            in_specs=[
                pl.BlockSpec((TOP, TOK), lambda i, p: (0, 0)),
                pl.BlockSpec((experts, 1, PACK, LANES), lambda i, p: (0, p[0] if own else 1 - p[0], 0, 0)),
                *[STAYS] * len(after),
            ],
            out_specs=pl.BlockSpec((TOK, D), lambda i, p: (0, 0)),
        ),
        out_shape=jax.ShapeDtypeStruct((TOK, D), dtype),
        compiler_params=params(),
        cost_estimate=cost(ROWS * TOK * D, (ROWS + 2 * TOK) * D),
    )(plane, routes, packed.reshape(experts, 2, PACK, LANES), *after)


def finish_kernel(near_ref, far_ref, after_ref, out_ref):
    out_ref[...] = (near_ref[...] + far_ref[...].astype(F32)) * 0.25


def finish(near, far, rows, after):
    height, breadth = far.shape
    part = pl.BlockSpec((rows, breadth), lambda i: (i, 0))
    return pl.pallas_call(
        finish_kernel,
        grid=(height // rows,),
        out_shape=jax.ShapeDtypeStruct((height, breadth), F32),
        in_specs=[part, part, STAYS],
        out_specs=part,
        compiler_params=params(),
        cost_estimate=cost(2 * height * breadth, 10 * height * breadth),
    )(near, far, after)


def near_kernel(kept_ref, got_ref, after_ref, out_ref):
    out_ref[...] = kept_ref[0] + got_ref[0].astype(F32)


def near_sum(kept, got, rows, after):
    _, height, breadth = kept.shape
    first = pl.BlockSpec((1, rows, breadth), lambda i: (0, i, 0))
    return pl.pallas_call(
        near_kernel,
        grid=(height // rows,),
        out_shape=jax.ShapeDtypeStruct((height, breadth), F32),
        in_specs=[first, first, STAYS],
        out_specs=pl.BlockSpec((rows, breadth), lambda i: (i, 0)),
        compiler_params=params(),
        cost_estimate=cost(height * breadth, 10 * height * breadth),
    )(kept, got, after)


def combine_output_kernel(
    routes_ref, probs_ref, cotangent_ref, packed_ref, after_in, after_out,
    out_ref, grad_ref, same_routes_ref, rows_ref,
):
    routes = place(routes_ref[...])
    same_routes_ref[...] = routes_ref[...]
    unpack_rows(packed_ref, rows_ref)
    key = slot_keys(routes)
    pick, last_pick = combine_tables(key, expert_weights(routes, probs_ref[...]))
    for j in range(D // 256):
        cut = slice(j * 256, (j + 1) * 256)
        total = dot(pick, rows_ref[:BIG, cut]) + dot(last_pick, rows_ref[BIG:, cut])
        out_ref[:, cut] = total.astype(BF16)
    main = dot_nt(rows_ref[:BIG, :], cotangent_ref[...])
    last = dot_nt(rows_ref[BIG:, :], cotangent_ref[...])
    for k in range(TOP):
        expert = routes[k : k + 1, :]
        slot = jnp.sum(jnp.where(expert == iota((LANES, TOK), 0), key, 0.0), axis=0, keepdims=True)
        slot = slot.astype(jnp.int32)
        row = jnp.where(slot < MAIN, expert * MAIN + slot, -1)
        value = jnp.sum(jnp.where(iota((BIG, TOK), 0) == row, main, 0.0), axis=0, keepdims=True)
        row = jnp.where(slot < MAIN, -1, expert)
        value += jnp.sum(jnp.where(iota((BLOCKS, TOK), 0) == row, last, 0.0), axis=0, keepdims=True)
        grad_ref[k : k + 1, :] = value


def combine_output(routes, probs, cotangent, packed, after):
    return pl.pallas_call(
        combine_output_kernel,
        out_shape=(
            jax.ShapeDtypeStruct((TOK, D), BF16),
            jax.ShapeDtypeStruct((TOP, TOK), F32),
            jax.ShapeDtypeStruct((TOP, TOK), jnp.int32),
        ),
        in_specs=[pl.BlockSpec(memory_space=pltpu.VMEM)] * 4 + [STAYS, STAYS],
        scratch_shapes=[pltpu.VMEM((ROWS, D), BF16)],
        compiler_params=params(),
        cost_estimate=cost(4 * ROWS * TOK * D, 2 * (ROWS + 2 * TOK) * D),
    )(routes, probs, cotangent, packed, *after)


def exchange(value):
    return lax.all_to_all(
        value, "expert", split_axis=0, concat_axis=0, tiled=True, axis_index_groups=[ORDER]
    )


def exchange_in_plane(value):
    planes = [PLANE_ORDER[z::2] for z in range(2)]
    value = value.reshape(BLOCKS // 2, 2 * PACK, LANES)
    return lax.all_to_all(
        value, "expert", split_axis=0, concat_axis=0, tiled=True, axis_index_groups=planes
    )


def between_planes(value):
    return lax.ppermute(value, "expert", [(e, e ^ 1) for e in range(BLOCKS)])


def across(value, flip):
    pairs = [(s * BLOCKS + e, (s ^ flip) * BLOCKS + e) for s in range(4) for e in range(BLOCKS)]
    return lax.ppermute(value, ("sample", "expert"), pairs)


def shards(tokens, routes, probs, cotangent, w_gate_up, w_down, gu_noise, down_noise):
    routes, probs, cotangent = routes[0].T, probs[0].T, cotangent[0]
    gu_noise, down_noise = gu_noise[0, 0], down_noise[0, 0]
    sample = lax.axis_index("sample")
    ours = jnp.stack([sample, sample ^ 2]).astype(jnp.int32)
    theirs = ours ^ 1

    send_x, send_dy = dispatch(routes, probs, tokens[0], cotangent)
    recv_x = exchange(send_x)
    weight_in = noisy(w_gate_up[0], gu_noise, recv_x)
    weight_out = noisy(w_down[0], down_noise, recv_x)
    recv_dy = exchange(send_dy)
    rows_x, gate, up, hidden = gate_up(recv_x, weight_in)
    output = down(hidden, weight_out)
    back_y = exchange(output)
    rows_dy, gate_grad, up_grad = mix(recv_dy, weight_out, gate, up, output)

    sent_in = weight_in_grads(theirs, gu_noise, rows_x, gate_grad, up_grad, BF16, output)
    got_in = across(sent_in, 1)
    sent_out = weight_out_grads(theirs, down_noise, hidden, rows_dy, BF16)
    got_out = across(sent_out, 1)
    kept_in = weight_in_grads(ours, gu_noise, rows_x, gate_grad, up_grad, F32, output)
    kept_out = weight_out_grads(ours, down_noise, hidden, rows_dy, F32)
    half_in = (kept_in[1] + got_in[1].astype(F32)).astype(BF16)
    half_out = (kept_out[1] + got_out[1].astype(F32)).astype(BF16)
    far_in = across(half_in, 2)
    far_out = across(half_out, 2)
    send_dx = input_grads(gate_grad, up_grad, weight_in, (half_in, half_out))
    back_dx = exchange_in_plane(send_dx)

    near_in = near_sum(kept_in, got_in, 256, back_y)
    near_out = near_sum(kept_out, got_out, 384, back_y)
    layer_out, prob_grad, same_routes = combine_output(
        routes, probs, cotangent, back_y, (near_in, near_out)
    )
    far_routes = between_planes(same_routes)
    plane = (lax.axis_index("expert") % 2).astype(jnp.int32)[None]
    there = combine(plane, False, far_routes, back_dx, BF16, ())
    here = combine(plane, True, routes, back_dx, F32, (there,))
    grad_in = finish(near_in, far_in, 256, there)
    grad_out = finish(near_out, far_out, 384, there)
    input_grad = (here + between_planes(there).astype(F32)).astype(BF16)
    return (layer_out[None], input_grad[None], prob_grad.T[None], grad_in[None], grad_out[None])


def solution(mesh):
    tokens = P("sample", "expert", None)
    noise = P("sample", "expert", None, None)
    experts = P("expert", None, None)
    in_specs = (tokens, tokens, tokens, tokens, experts, experts, noise, noise)
    out_specs = (tokens, tokens, tokens, P("expert", "sample", None), P("expert", None, "sample"))
    return jax.shard_map(shards, mesh=mesh, in_specs=in_specs, out_specs=out_specs, check_vma=False)
```
